256 devices in a mesh: gx: 8 (over y, core), gy: 8 (over z_hi, x), af: 4 (over z_lo).
Axes of the slice: x: 4, y: 4, z: 8 (z_hi: 2, z_lo: 4; z = z_hi * 4 + z_lo), core: 2. Of those that a mesh axis runs over, the one named last changes fastest.
Arguments:
- volume: bfloat16 [32, 32, 128, 128], P('af', 'gx', 'gy'), may hold values from -6 to 6
- weight_one: bfloat16 [32, 32, 3, 3, 3], P('af'), may hold values from -0.21875 to 0.21875
- bias_one: float32 [32], P('af'), may hold values from -1 to 1
- weight_two: bfloat16 [32, 32, 3, 3, 3], P('af'), may hold values from -0.21875 to 0.21875
- cotangent: bfloat16 [32, 32, 128, 128], P('af', 'gx', 'gy'), may hold values from -6 to 6
Outputs:
- output: bfloat16 [32, 32, 128, 128], P('af', 'gx', 'gy')
- input_grad: bfloat16 [32, 32, 128, 128], P('af', 'gx', 'gy')
- grad_one: float32 [32, 32, 3, 3, 3], P('af')
- bias_grad: float32 [32], P('af')
- grad_two: float32 [32, 32, 3, 3, 3], P('af')
The draws below stay inside these ranges and needn't reach their ends.
All inputs are finite; a program needn't handle non-finite values.
Results may differ from the reference program's by a relative error of at most 0.0065.
Values may be sent and summed in bfloat16 or wider, within the bound.
A program may use at most 64 MiB of HBM per device.

```python
import jax
import jax.numpy as jnp
from jax import lax

C = 32
NZ = 128
NX = 32
NY = 128


def shard_levels(rng, extent, pieces, least, largest):
    gain = 1.0
    for dim, blocks in pieces:
        draws = jax.random.uniform(jax.random.fold_in(jax.random.fold_in(rng, 6), dim), (blocks,), jnp.float32, least / len(pieces), largest / len(pieces))
        gain = gain * jnp.repeat(jnp.exp(draws), extent[dim] // blocks).reshape((-1,) + (1,) * (len(extent) - 1 - dim))
    return gain


def scatter_about(key, dims, width, limit, cuts=(), kind=jnp.bfloat16):
    factor_of = shard_levels(key, dims, cuts, -0.22, 0.18) if cuts else 1.0
    result = jax.random.normal(key, dims, jnp.float32) * width * factor_of
    return jnp.minimum(jnp.maximum(result, -limit), limit).astype(kind)


def setup_inputs(seed: int = 0) -> dict:
    seeds = jax.random.split(jax.random.key(seed), 6)
    volume = scatter_about(seeds[0], (C, NX, NY, NZ), 1.0, 6.0, ((0, 4), (1, 8), (2, 8)))
    weight_one = scatter_about(seeds[1], (C, C, 3, 3, 3), (27 * C) ** -0.5, 0.21875, ((0, 4),))
    bias_one = jnp.clip(jax.random.uniform(seeds[2], (C,), jnp.float32, -1.0, 1.0) * shard_levels(seeds[2], (C,), ((0, 4),), -0.4, 0.0), -1.0, 1.0)
    weight_two = scatter_about(seeds[3], (C, C, 3, 3, 3), (27 * C) ** -0.5, 0.21875, ((0, 4),))
    cotangent = scatter_about(seeds[4], (C, NX, NY, NZ), 1.0, 6.0, ((0, 4), (1, 8), (2, 8)))
    return dict(volume=volume, weight_one=weight_one, bias_one=bias_one, weight_two=weight_two, cotangent=cotangent)


def conv_full(padded, weight):
    conv_out = lax.conv_general_dilated(padded[None], weight, (1, 1, 1), 'VALID', dimension_numbers=('NCDHW', 'OIDHW', 'NCDHW'), precision=lax.Precision.HIGHEST)
    return conv_out[0]

def pad_all(values):
    return jnp.pad(values, ((0, 0), (1, 1), (1, 1), (1, 1)))

def flipped(weight):
    return jnp.transpose(jnp.flip(weight, (2, 3, 4)), (1, 0, 2, 3, 4))

def kernel_grad(padded, cot_field):
    chans = cot_field.shape[0]
    size_x, size_y, size_z = (cot_field.shape[1], cot_field.shape[2], cot_field.shape[3])
    flat_cot = cot_field.reshape(chans, -1)
    blocks = []
    for off_x in range(3):
        for off_y in range(3):
            for off_z in range(3):
                window = padded[:, off_x:off_x + size_x, off_y:off_y + size_y, off_z:off_z + size_z]
                flat_win = window.reshape(padded.shape[0], -1)
                blocks.append(jnp.dot(flat_cot, flat_win.T, precision=lax.Precision.HIGHEST))
    stacked = jnp.stack(blocks, axis=-1)
    return stacked.reshape(chans, padded.shape[0], 3, 3, 3)

def reference(volume, weight_one, bias_one, weight_two, cotangent):
    first_w = weight_one.astype(jnp.float32)
    second_w = weight_two.astype(jnp.float32)
    vol_pad = pad_all(volume.astype(jnp.float32))
    pre_act = conv_full(vol_pad, first_w) + bias_one[:, None, None, None]
    hidden = jax.nn.silu(pre_act).astype(jnp.bfloat16)
    hid_pad = pad_all(hidden.astype(jnp.float32))
    output = conv_full(hid_pad, second_w).astype(jnp.bfloat16)
    cot_f = cotangent.astype(jnp.float32)
    scaling = 1.0 / jnp.sqrt(jnp.float32(NX * NY * NZ))
    grad_two = kernel_grad(hid_pad, cot_f) * scaling
    hidden_grad = conv_full(pad_all(cot_f), flipped(second_w))
    sigma_vals = jax.nn.sigmoid(pre_act)
    pre_grad = (hidden_grad * sigma_vals * (1.0 + pre_act * (1.0 - sigma_vals))).astype(jnp.bfloat16)
    pre_f = pre_grad.astype(jnp.float32)
    grad_one = kernel_grad(vol_pad, pre_f) * scaling
    bias_grad = lax.optimization_barrier(jnp.sum(pre_f, axis=(1, 2, 3))) * scaling
    input_grad = conv_full(pad_all(pre_f), flipped(first_w)).astype(jnp.bfloat16)
    return (output, input_grad, grad_one, bias_grad, grad_two)
```

```python
import functools
import math

import jax
import jax.numpy as jnp
from jax import lax
from jax.experimental import pallas as pl
from jax.experimental.pallas import tpu as pltpu
from jax.sharding import PartitionSpec as P

MESH = pl.DeviceIdType.MESH
F32 = jnp.float32
BF16 = jnp.bfloat16

VOL, COT, HID, PRE = 0, 1, 2, 3
SIDES = [(dx, dy) for dx in (-1, 0, 1) for dy in (-1, 0, 1) if (dx, dy) != (0, 0)]
SEND = {-1: (1, 1), 0: (1, 4), 1: (4, 1)}
LAND = {-1: (5, 1), 0: (1, 4), 1: (0, 1)}


def iota(shape, dim):
    return lax.broadcasted_iota(jnp.int32, shape, dim)


def kernel(
    dims,
    vol, w_one, bias, w_two, cot,
    out, in_grad, g_one, g_bias, g_two,
    stage, got, w_stage, w_got, field, pre_act, lhs,
    out_stage, out_got, grad, core_got, core_sum, z_got, y_got, x_got, h_stage, h_got, final,
    in_send, in_recv, w_send, w_recv, halo_send, halo_recv, out_send, out_recv,
    core_send, core_recv, z_send, z_recv, y_send, y_recv, x_send, x_recv, h_send, h_recv,
):
    n_gx, n_gy = dims
    n_y, n_x = n_gx // 2, n_gy // 2
    gx, gy, af = lax.axis_index("gx"), lax.axis_index("gy"), lax.axis_index("af")
    row, core = gx // 2, gx % 2
    col, high = gy % n_x, gy // n_x

    def turned(at):
        even = (at % 2) == 0
        upper = at >= n_x
        return jnp.logical_xor(even, upper)

    def sub_of(at_af, at_gy):
        return jnp.where(turned(at_gy), 3 - at_af, at_af)

    sub = sub_of(af, gy)

    def y_neighbour(step):
        if step == 0:
            return gy, af
        inside = (sub < 3) if step > 0 else (sub > 0)
        gy_new = jnp.where(inside, gy, gy + step)
        sub_new = jnp.where(inside, sub + step, 0 if step > 0 else 3)
        return gy_new, sub_of(sub_new, gy_new)

    def has(dx, dy):
        checks = []
        if dx < 0:
            checks.append(gx > 0)
        if dx > 0:
            checks.append(gx < n_gx - 1)
        if dy < 0:
            checks.append(jnp.logical_or(gy > 0, sub > 0))
        if dy > 0:
            checks.append(jnp.logical_or(gy < n_gy - 1, sub < 3))
        if len(checks) == 1:
            return checks[0]
        return jnp.logical_and(checks[0], checks[1])

    neighbour = {}
    for dx, dy in SIDES:
        gy_new, af_new = y_neighbour(dy)
        neighbour[dx, dy] = {"gx": gx + dx, "gy": gy_new, "af": af_new}
    af_peer = [(af + k) % 4 for k in range(4)]

    zero_row = jnp.zeros((4, 6, 32, 128), BF16)
    for x in (0, 5):
        field[:, x] = zero_row
    for x in range(1, 5):
        for y in (0, 5):
            field[:, x, y] = jnp.zeros((4, 32, 128), BF16)
    grad[...] = jnp.zeros(grad.shape, F32)

    barrier = pltpu.get_barrier_semaphore()
    partners = [{"af": af_peer[k]} for k in range(1, 4)]
    partners += [{"gx": 2 * row + 1 - core}]
    partners += [{"gx": 2 * ((row + k) % n_y) + core} for k in range(1, n_y)]
    partners += [{"gy": high * n_x + (col + k) % n_x} for k in range(1, n_x)]
    partners += [{"gy": (1 - high) * n_x + col}]
    for partner in partners:
        pl.semaphore_signal(barrier, inc=1, device_id=partner, device_id_type=MESH)
    expected = jnp.int32(len(partners))
    for side in SIDES:

        @pl.when(has(*side))
        def _(side=side):
            pl.semaphore_signal(barrier, inc=1, device_id=neighbour[side], device_id_type=MESH)

        expected = expected + has(*side).astype(jnp.int32)

    r, q = iota((128, 128), 0), iota((128, 128), 1)
    to_wire = jnp.where(q == (r % 8) * 16 + r // 8, 1.0, 0.0).astype(BF16)
    from_wire = jnp.where(q == (r % 16) * 8 + r // 16, 1.0, 0.0).astype(BF16)

    def stage_input(which, source):
        block = jnp.concatenate([source[:, x].reshape(128, 128) for x in range(4)], axis=1)
        moved = jnp.dot(to_wire, block, preferred_element_type=F32).astype(BF16)
        for x in range(4):
            for j in range(4):
                part = moved[32 * j : 32 * j + 32, 128 * x : 128 * x + 128]
                stage[which, j, x] = part.reshape(2, 16, 128)
        got[which, pl.ds(af, 1)] = stage[which, pl.ds(sub, 1)]

    def in_copy(which, k):
        return pltpu.make_async_remote_copy(
            src_ref=stage.at[which, sub_of(af_peer[k], gy)],
            dst_ref=got.at[which, af],
            send_sem=in_send.at[which, k],
            recv_sem=in_recv.at[which, k],
            device_id={"af": af_peer[k]},
            device_id_type=MESH,
        )

    def w_copy(k):
        return pltpu.make_async_remote_copy(
            src_ref=w_stage,
            dst_ref=w_got.at[af],
            send_sem=w_send.at[k],
            recv_sem=w_recv.at[k],
            device_id={"af": af_peer[k]},
            device_id_type=MESH,
        )

    stage_input(VOL, vol)
    pl.semaphore_wait(barrier, expected)
    for k in (2, 1, 3):
        in_copy(VOL, k).start()

    diag = iota((8, 8), 0) == iota((8, 8), 1)
    bias_col = jnp.sum(jnp.where(diag, bias[...], 0.0), axis=1, keepdims=True)
    part_a = bias_col.astype(BF16).astype(F32)
    part_b = (bias_col - part_a).astype(BF16).astype(F32)
    part_c = (bias_col - part_a) - part_b
    lane32 = iota((8, 32), 1)
    spare = jnp.where(lane32 == 0, part_a, jnp.where(lane32 == 1, part_b, jnp.where(lane32 == 2, part_c, 0.0)))
    for which, weight in enumerate((w_one, w_two)):
        groups = []
        for a in range(7):
            taps = []
            for b in range(4):
                t = 4 * a + b
                taps.append(weight[t // 9, (t // 3) % 3, t % 3].astype(F32) if t < 27 else spare)
            groups.append(jnp.concatenate(taps, axis=1))
        groups.append(jnp.zeros((8, 128), F32))
        packed = jnp.concatenate(groups, axis=0).astype(BF16)
        w_stage[which] = packed
        w_got[af, which] = packed
    for k in (2, 1, 3):
        w_copy(k).start()
    stage_input(COT, cot)
    for k in (2, 1, 3):
        in_copy(COT, k).start()

    def halo_copy(which, side):
        number = SIDES.index(side)
        (sx, nx), (sy, ny) = SEND[side[0]], SEND[side[1]]
        (lx, _), (ly, _) = LAND[side[0]], LAND[side[1]]
        return pltpu.make_async_remote_copy(
            src_ref=field.at[which, sx : sx + nx, sy : sy + ny],
            dst_ref=field.at[which, lx : lx + nx, ly : ly + ny],
            send_sem=halo_send.at[which, number],
            recv_sem=halo_recv.at[which, number],
            device_id=neighbour[side],
            device_id_type=MESH,
        )

    def halo_start(which):
        for side in SIDES:

            @pl.when(has(*side))
            def _(side=side):
                halo_copy(which, side).start()

    def halo_wait(which):
        for side in SIDES:

            @pl.when(has(-side[0], -side[1]))
            def _(side=side):
                halo_copy(which, side).wait_recv()

    def assemble(which):
        for x in range(4):
            for pair in range(2):
                parts = [got[which, s, x, pair].astype(F32) for s in range(4)]
                for odd in range(2):
                    rows = [part[8 * odd : 8 * odd + 8] for part in parts]
                    field[which, 1 + x, 1 + 2 * pair + odd] = jnp.concatenate(rows, axis=0).astype(BF16)

    for k in range(1, 4):
        in_copy(VOL, k).wait_recv()
    assemble(VOL)
    halo_start(VOL)

    for k in range(1, 4):
        w_copy(k).wait_recv()

    def taps_of(which):
        parts = [w_got[s, which].astype(F32) for s in range(4)]
        groups = [
            jnp.concatenate([part[8 * a : 8 * a + 8] for part in parts], axis=0) for a in range(7)
        ]

        def tap(dx, dy, dz):
            t = (dx * 3 + dy) * 3 + dz
            return groups[t // 4][:, 32 * (t % 4) : 32 * (t % 4) + 32]

        return groups, tap

    def make_forward(which):
        groups, tap = taps_of(which)
        for dz in range(3):
            line = jnp.concatenate([tap(k // 3, k % 3, dz) for k in range(9)], axis=1)
            lhs[2 * which, 32 * dz : 32 * dz + 32] = line.astype(BF16)
        return groups

    def make_turned(which):
        _, tap = taps_of(which)
        zeros = jnp.zeros((32, 32), F32)
        for dx in range(3):
            lines = [
                jnp.concatenate([tap(2 - dx, 2 - dy, 2 - dz) for dz in range(3)] + [zeros], axis=1)
                for dy in range(3)
            ]
            lines.append(jnp.zeros((32, 128), F32))
            block = jnp.concatenate(lines, axis=0)
            lhs[2 * which + 1, :, 96 * dx : 96 * dx + 96] = block.T[:96, :96].astype(BF16)

    groups = make_forward(0)
    bias_all = groups[6][:, 96:97] + groups[6][:, 97:98] + groups[6][:, 98:99]
    make_turned(1)

    lane = iota((32, 128), 1)
    not_first = lane > 0
    not_last = lane < 127

    def shift_up(rows):
        return jnp.where(not_first, pltpu.roll(rows, 1, 1), 0.0)

    def shift_down(rows):
        return jnp.where(not_last, pltpu.roll(rows, 127, 1), 0.0)

    def window(which, x, dx):
        return jnp.concatenate(
            [field[which, x + dx, y : y + 3].reshape(96, 128) for y in range(4)], axis=1
        )

    def conv(which, number, x):
        block = jnp.concatenate([window(which, x, dx) for dx in range(3)], axis=0)
        sums = jnp.dot(lhs[number], block, preferred_element_type=F32)
        lines = []
        for y in range(4):
            part = sums[:, 128 * y : 128 * y + 128]
            lines.append(part[32:64] + shift_up(part[0:32]) + shift_down(part[64:96]))
        return lines

    halo_wait(VOL)
    for x in range(4):
        for y, line in enumerate(conv(VOL, 0, x)):
            act = line + bias_all
            pre_act[x, y] = act
            field[HID, 1 + x, 1 + y] = (act / (1.0 + jnp.exp(-act))).astype(BF16)
    halo_start(HID)

    for k in range(1, 4):
        in_copy(COT, k).wait_recv()
    assemble(COT)
    halo_start(COT)
    make_forward(1)
    make_turned(0)
    halo_wait(COT)
    bias_sum = jnp.zeros((32, 128), F32)
    for x in range(4):
        for y, line in enumerate(conv(COT, 3, x)):
            act = pre_act[x, y]
            sig = 1.0 / (1.0 + jnp.exp(-act))
            value = (line * sig * (1.0 + act * (1.0 - sig))).astype(BF16)
            bias_sum = bias_sum + value.astype(F32)
            field[PRE, 1 + x, 1 + y] = value
    halo_start(PRE)

    def shifted(which, x, flip):
        columns = []
        for y in range(4):
            rows = field[which, 1 + x, 1 + y].astype(F32)
            up, down = shift_up(rows), shift_down(rows)
            trio = [down, rows, up] if flip else [up, rows, down]
            columns.append(jnp.concatenate(trio, axis=0).astype(BF16))
        return jnp.concatenate(columns, axis=1)

    along = (((1,), (1,)), ((), ()))

    acc_one = [jnp.zeros((96, 96), F32) for _ in range(3)]
    acc_two = [jnp.zeros((96, 96), F32) for _ in range(3)]
    for x in range(4):
        own_pre = shifted(PRE, x, True)
        own_hid = shifted(HID, x, False)
        for dx in range(3):
            acc_one[dx] = acc_one[dx] + lax.dot_general(
                own_pre, window(VOL, x, dx), along, preferred_element_type=F32
            )
            acc_two[dx] = acc_two[dx] + lax.dot_general(
                window(COT, x, dx), own_hid, along, preferred_element_type=F32
            )
    bias_own = jnp.sum(bias_sum, axis=1, keepdims=True)
    for dx in range(3):
        for k in range(3):
            for s in range(4):
                rows = slice(32 * k + 8 * s, 32 * k + 8 * s + 8)
                grad[0, s, 3 * dx + k, :, 0:96] = acc_one[dx][rows]
                grad[1, s, 3 * dx + k, :, 0:96] = acc_two[dx][rows]
    for s in range(4):
        grad[0, s, 0, :, 96:97] = bias_own[8 * s : 8 * s + 8]

    core_copy = pltpu.make_async_remote_copy(
        src_ref=grad.at[1 - core],
        dst_ref=core_got,
        send_sem=core_send.at[0],
        recv_sem=core_recv.at[0],
        device_id={"gx": 2 * row + 1 - core},
        device_id_type=MESH,
    )
    core_copy.start()

    def out_copy(which, k):
        return pltpu.make_async_remote_copy(
            src_ref=out_stage.at[which, af_peer[k]],
            dst_ref=out_got.at[which, sub],
            send_sem=out_send.at[which, k],
            recv_sem=out_recv.at[which, k],
            device_id={"af": af_peer[k]},
            device_id_type=MESH,
        )

    def produce(which, source, number):
        for x in range(4):
            lines = conv(source, number, x)
            for pair in range(2):
                for s in range(4):
                    rows = [lines[2 * pair + odd][8 * s : 8 * s + 8] for odd in range(2)]
                    out_stage[which, s, x, pair] = jnp.concatenate(rows, axis=0).astype(BF16)
        out_got[which, pl.ds(sub, 1)] = out_stage[which, pl.ds(af, 1)]
        for k in (2, 1, 3):
            out_copy(which, k).start()

    halo_wait(HID)
    produce(0, HID, 2)

    core_copy.wait_recv()
    core_sum[...] = grad[core] + core_got[...]
    z_got[af] = core_sum[af]

    def z_copy(k):
        return pltpu.make_async_remote_copy(
            src_ref=core_sum.at[af_peer[k]],
            dst_ref=z_got.at[af],
            send_sem=z_send.at[k],
            recv_sem=z_recv.at[k],
            device_id={"af": af_peer[k]},
            device_id_type=MESH,
        )

    for k in range(1, 4):
        z_copy(k).start()

    halo_wait(PRE)
    produce(1, PRE, 1)

    for k in range(1, 4):
        z_copy(k).wait_recv()
    y_got[row] = z_got[0] + z_got[1] + z_got[2] + z_got[3]

    def y_copy(k):
        return pltpu.make_async_remote_copy(
            src_ref=y_got.at[row],
            dst_ref=y_got.at[row],
            send_sem=y_send.at[k],
            recv_sem=y_recv.at[k],
            device_id={"gx": 2 * ((row + k) % n_y) + core},
            device_id_type=MESH,
        )

    for k in range(1, n_y):
        y_copy(k).start()
    for k in range(1, n_y):
        y_copy(k).wait_recv()
    x_got[col] = sum([y_got[i] for i in range(1, n_y)], y_got[0])

    def x_copy(k):
        return pltpu.make_async_remote_copy(
            src_ref=x_got.at[col],
            dst_ref=x_got.at[col],
            send_sem=x_send.at[k],
            recv_sem=x_recv.at[k],
            device_id={"gy": high * n_x + (col + k) % n_x},
            device_id_type=MESH,
        )

    for k in range(1, n_x):
        x_copy(k).start()
    for k in range(1, n_x):
        x_copy(k).wait_recv()
    h_stage[...] = sum([x_got[i] for i in range(1, n_x)], x_got[0])
    h_copy = pltpu.make_async_remote_copy(
        src_ref=h_stage,
        dst_ref=h_got,
        send_sem=h_send.at[0],
        recv_sem=h_recv.at[0],
        device_id={"gy": (1 - high) * n_x + col},
        device_id_type=MESH,
    )
    h_copy.start()

    def finish(which, target):
        for k in range(1, 4):
            out_copy(which, k).wait_recv()
        block = jnp.concatenate(
            [
                jnp.concatenate([out_got[which, j, x].reshape(32, 128) for j in range(4)], axis=0)
                for x in range(4)
            ],
            axis=1,
        )
        moved = jnp.dot(from_wire, block, preferred_element_type=F32).astype(BF16)
        for x in range(4):
            target[:, x] = moved[:, 128 * x : 128 * x + 128].reshape(8, 16, 128)

    finish(0, out)
    h_copy.wait_recv()
    scale = 1.0 / math.sqrt(4 * n_gx * 16 * n_gy * 128)
    final[core] = (h_stage[...] + h_got[...]) * scale
    last_copy = pltpu.make_async_remote_copy(
        src_ref=final.at[core],
        dst_ref=final.at[core],
        send_sem=core_send.at[1],
        recv_sem=core_recv.at[1],
        device_id={"gx": 2 * row + 1 - core},
        device_id_type=MESH,
    )
    last_copy.start()
    finish(1, in_grad)
    last_copy.wait_recv()
    for dx in range(3):
        for k in range(3):
            tile_one = final[0, 3 * dx + k]
            tile_two = final[1, 3 * dx + k]
            for m in range(3):
                g_one[dx, m, k] = tile_one[:, 32 * m : 32 * m + 32]
                g_two[2 - dx, 2 - k, m] = tile_two[:, 32 * m : 32 * m + 32]
    g_bias[...] = final[0, 0][:, 96:97]

    for k in range(1, 4):
        in_copy(VOL, k).wait_send()
        in_copy(COT, k).wait_send()
        w_copy(k).wait_send()
        out_copy(0, k).wait_send()
        out_copy(1, k).wait_send()
        z_copy(k).wait_send()
    for which in (VOL, COT, HID, PRE):
        for side in SIDES:

            @pl.when(has(*side))
            def _(which=which, side=side):
                halo_copy(which, side).wait_send()

    core_copy.wait_send()
    for k in range(1, n_y):
        y_copy(k).wait_send()
    for k in range(1, n_x):
        x_copy(k).wait_send()
    h_copy.wait_send()
    last_copy.wait_send()


def body(dims, volume, weight_one, bias_one, weight_two, cotangent):
    n_y, n_x = dims[0] // 2, dims[1] // 2
    as_taps = (2, 3, 4, 0, 1)
    dma = pltpu.SemaphoreType.DMA
    out, in_grad, g_one, g_bias, g_two = pl.pallas_call(
        functools.partial(kernel, dims),
        out_shape=(
            jax.ShapeDtypeStruct((8, 4, 16, 128), BF16),
            jax.ShapeDtypeStruct((8, 4, 16, 128), BF16),
            jax.ShapeDtypeStruct((3, 3, 3, 8, 32), F32),
            jax.ShapeDtypeStruct((8, 1), F32),
            jax.ShapeDtypeStruct((3, 3, 3, 8, 32), F32),
        ),
        in_specs=[pl.BlockSpec(memory_space=pltpu.VMEM)] * 5,
        out_specs=[pl.BlockSpec(memory_space=pltpu.VMEM)] * 5,
        scratch_shapes=[
            pltpu.VMEM((2, 4, 4, 2, 16, 128), BF16),
            pltpu.VMEM((2, 4, 4, 2, 16, 128), BF16),
            pltpu.VMEM((2, 64, 128), BF16),
            pltpu.VMEM((4, 2, 64, 128), BF16),
            pltpu.VMEM((4, 6, 6, 32, 128), BF16),
            pltpu.VMEM((4, 4, 32, 128), F32),
            pltpu.VMEM((4, 96, 288), BF16),
            pltpu.VMEM((2, 4, 4, 2, 16, 128), BF16),
            pltpu.VMEM((2, 4, 4, 2, 16, 128), BF16),
            pltpu.VMEM((2, 4, 9, 8, 128), F32),
            pltpu.VMEM((4, 9, 8, 128), F32),
            pltpu.VMEM((4, 9, 8, 128), F32),
            pltpu.VMEM((4, 9, 8, 128), F32),
            pltpu.VMEM((n_y, 9, 8, 128), F32),
            pltpu.VMEM((n_x, 9, 8, 128), F32),
            pltpu.VMEM((9, 8, 128), F32),
            pltpu.VMEM((9, 8, 128), F32),
            pltpu.VMEM((2, 9, 8, 128), F32),
            dma((2, 4)), dma((2, 4)), dma((4,)), dma((4,)), dma((4, 8)), dma((4, 8)), dma((2, 4)), dma((2, 4)),
            dma((2,)), dma((2,)), dma((4,)), dma((4,)), dma((4,)), dma((4,)), dma((4,)), dma((4,)), dma((1,)), dma((1,)),
        ],
        compiler_params=pltpu.CompilerParams(
            collective_id=0, has_side_effects=True, vmem_limit_bytes=32 * 1024 * 1024
        ),
    )(
        volume,
        jnp.transpose(weight_one, as_taps),
        bias_one.reshape(1, 8),
        jnp.transpose(weight_two, as_taps),
        cotangent,
    )
    as_given = (3, 4, 0, 1, 2)
    return (
        out,
        in_grad,
        jnp.transpose(g_one, as_given),
        g_bias.reshape(8),
        jnp.transpose(g_two, as_given),
    )


def solution(mesh):
    dims = (mesh.shape["gx"], mesh.shape["gy"])
    return jax.shard_map(
        functools.partial(body, dims),
        mesh=mesh,
        in_specs=(
            P("af", "gx", "gy", None),
            P("af", None, None, None, None),
            P("af"),
            P("af", None, None, None, None),
            P("af", "gx", "gy", None),
        ),
        out_specs=(
            P("af", "gx", "gy", None),
            P("af", "gx", "gy", None),
            P("af", None, None, None, None),
            P("af"),
            P("af", None, None, None, None),
        ),
        check_vma=False,
    )
```

```python
import functools
import math

import jax
import jax.numpy as jnp
from jax import lax
from jax.experimental import pallas as pl
from jax.experimental.pallas import tpu as pltpu
from jax.sharding import PartitionSpec as P

MESH = pl.DeviceIdType.MESH
F32 = jnp.float32
BF16 = jnp.bfloat16

VOL, COT, HID, PRE = 0, 1, 2, 3
SIDES = [(dx, dy) for dx in (-1, 0, 1) for dy in (-1, 0, 1) if (dx, dy) != (0, 0)]
SEND = {-1: (1, 1), 0: (1, 4), 1: (4, 1)}
LAND = {-1: (5, 1), 0: (1, 4), 1: (0, 1)}


def iota(shape, dim):
    return lax.broadcasted_iota(jnp.int32, shape, dim)


def kernel(
    dims,
    vol_in, w_one_in, bias_in, w_two_in, cot_in,
    out_to, in_grad_to, g_one_to, g_bias_to, g_two_to,
    out, in_grad, g_one, g_bias, g_two,
    vol, w_one, bias, w_two, cot,
    stage, got, w_stage, w_got, field, pre_act, lhs,
    out_stage, out_got, grad, core_got, core_sum, z_got, y_got, x_got, h_stage, h_got, final,
    in_send, in_recv, w_send, w_recv, halo_send, halo_recv, out_send, out_recv,
    core_send, core_recv, z_send, z_recv, y_send, y_recv, x_send, x_recv, h_send, h_recv, load_sem, store_sem,
):
    loads = [
        pltpu.make_async_copy(source, target, load_sem.at[i])
        for i, (source, target) in enumerate(
            ((vol_in, vol), (w_one_in, w_one), (w_two_in, w_two), (bias_in, bias), (cot_in, cot))
        )
    ]
    for load in loads:
        load.start()
    stores = [
        pltpu.make_async_copy(source, target, store_sem.at[i])
        for i, (source, target) in enumerate(
            ((out, out_to), (in_grad, in_grad_to), (g_one, g_one_to), (g_bias, g_bias_to), (g_two, g_two_to))
        )
    ]
    n_gx, n_gy = dims
    n_y, n_x = n_gx // 2, n_gy // 2
    gx, gy, af = lax.axis_index("gx"), lax.axis_index("gy"), lax.axis_index("af")
    row, core = gx // 2, gx % 2
    col, high = gy % n_x, gy // n_x

    def turned(at):
        even = (at % 2) == 0
        upper = at >= n_x
        return jnp.logical_xor(even, upper)

    def sub_of(at_af, at_gy):
        return jnp.where(turned(at_gy), 3 - at_af, at_af)

    sub = sub_of(af, gy)

    def y_neighbour(step):
        if step == 0:
            return gy, af
        inside = (sub < 3) if step > 0 else (sub > 0)
        gy_new = jnp.where(inside, gy, gy + step)
        sub_new = jnp.where(inside, sub + step, 0 if step > 0 else 3)
        return gy_new, sub_of(sub_new, gy_new)

    def has(dx, dy):
        checks = []
        if dx < 0:
            checks.append(gx > 0)
        if dx > 0:
            checks.append(gx < n_gx - 1)
        if dy < 0:
            checks.append(jnp.logical_or(gy > 0, sub > 0))
        if dy > 0:
            checks.append(jnp.logical_or(gy < n_gy - 1, sub < 3))
        if len(checks) == 1:
            return checks[0]
        return jnp.logical_and(checks[0], checks[1])

    neighbour = {}
    for dx, dy in SIDES:
        gy_new, af_new = y_neighbour(dy)
        neighbour[dx, dy] = {"gx": gx + dx, "gy": gy_new, "af": af_new}
    af_peer = [(af + k) % 4 for k in range(4)]

    zero_row = jnp.zeros((4, 6, 32, 128), BF16)
    for x in (0, 5):
        field[:, x] = zero_row
    for x in range(1, 5):
        for y in (0, 5):
            field[:, x, y] = jnp.zeros((4, 32, 128), BF16)
    grad[...] = jnp.zeros(grad.shape, F32)

    barrier = pltpu.get_barrier_semaphore()
    partners = [{"af": af_peer[k]} for k in range(1, 4)]
    partners += [{"gx": 2 * row + 1 - core}]
    partners += [{"gx": 2 * ((row + k) % n_y) + core} for k in range(1, n_y)]
    partners += [{"gy": high * n_x + (col + k) % n_x} for k in range(1, n_x)]
    partners += [{"gy": (1 - high) * n_x + col}]
    for partner in partners:
        pl.semaphore_signal(barrier, inc=1, device_id=partner, device_id_type=MESH)
    expected = jnp.int32(len(partners))
    for side in SIDES:

        @pl.when(has(*side))
        def _(side=side):
            pl.semaphore_signal(barrier, inc=1, device_id=neighbour[side], device_id_type=MESH)

        expected = expected + has(*side).astype(jnp.int32)

    r, q = iota((128, 128), 0), iota((128, 128), 1)
    to_wire = jnp.where(q == (r % 8) * 16 + r // 8, 1.0, 0.0).astype(BF16)
    from_wire = jnp.where(q == (r % 16) * 8 + r // 16, 1.0, 0.0).astype(BF16)

    def stage_input(which, source):
        block = jnp.concatenate([source[:, x].reshape(128, 128) for x in range(4)], axis=1)
        moved = jnp.dot(to_wire, block, preferred_element_type=F32).astype(BF16)
        for x in range(4):
            for j in range(4):
                part = moved[32 * j : 32 * j + 32, 128 * x : 128 * x + 128]
                stage[which, j, x] = part.reshape(2, 16, 128)
        got[which, pl.ds(af, 1)] = stage[which, pl.ds(sub, 1)]

    def in_copy(which, k):
        return pltpu.make_async_remote_copy(
            src_ref=stage.at[which, sub_of(af_peer[k], gy)],
            dst_ref=got.at[which, af],
            send_sem=in_send.at[which, k],
            recv_sem=in_recv.at[which, k],
            device_id={"af": af_peer[k]},
            device_id_type=MESH,
        )

    def w_copy(k):
        return pltpu.make_async_remote_copy(
            src_ref=w_stage,
            dst_ref=w_got.at[af],
            send_sem=w_send.at[k],
            recv_sem=w_recv.at[k],
            device_id={"af": af_peer[k]},
            device_id_type=MESH,
        )

    loads[0].wait()
    stage_input(VOL, vol)
    pl.semaphore_wait(barrier, expected)
    for k in (2, 1, 3):
        in_copy(VOL, k).start()

    for load in loads[1:]:
        load.wait()
    diag = iota((8, 8), 0) == iota((8, 8), 1)
    bias_col = jnp.sum(jnp.where(diag, bias[...], 0.0), axis=1, keepdims=True)
    part_a = bias_col.astype(BF16).astype(F32)
    part_b = (bias_col - part_a).astype(BF16).astype(F32)
    part_c = (bias_col - part_a) - part_b
    lane32 = iota((8, 32), 1)
    spare = jnp.where(lane32 == 0, part_a, jnp.where(lane32 == 1, part_b, jnp.where(lane32 == 2, part_c, 0.0)))
    for which, weight in enumerate((w_one, w_two)):
        groups = []
        for a in range(7):
            taps = []
            for b in range(4):
                t = 4 * a + b
                taps.append(weight[t // 9, (t // 3) % 3, t % 3].astype(F32) if t < 27 else spare)
            groups.append(jnp.concatenate(taps, axis=1))
        groups.append(jnp.zeros((8, 128), F32))
        packed = jnp.concatenate(groups, axis=0).astype(BF16)
        w_stage[which] = packed
        w_got[af, which] = packed
    for k in (2, 1, 3):
        w_copy(k).start()
    stage_input(COT, cot)
    for k in (2, 1, 3):
        in_copy(COT, k).start()

    def halo_copy(which, side):
        number = SIDES.index(side)
        (sx, nx), (sy, ny) = SEND[side[0]], SEND[side[1]]
        (lx, _), (ly, _) = LAND[side[0]], LAND[side[1]]
        return pltpu.make_async_remote_copy(
            src_ref=field.at[which, sx : sx + nx, sy : sy + ny],
            dst_ref=field.at[which, lx : lx + nx, ly : ly + ny],
            send_sem=halo_send.at[which, number],
            recv_sem=halo_recv.at[which, number],
            device_id=neighbour[side],
            device_id_type=MESH,
        )

    def halo_start(which):
        for side in SIDES:

            @pl.when(has(*side))
            def _(side=side):
                halo_copy(which, side).start()

    def halo_wait(which):
        for side in SIDES:

            @pl.when(has(-side[0], -side[1]))
            def _(side=side):
                halo_copy(which, side).wait_recv()

    def assemble(which):
        for x in range(4):
            for pair in range(2):
                parts = [got[which, s, x, pair].astype(F32) for s in range(4)]
                for odd in range(2):
                    rows = [part[8 * odd : 8 * odd + 8] for part in parts]
                    field[which, 1 + x, 1 + 2 * pair + odd] = jnp.concatenate(rows, axis=0).astype(BF16)

    for k in range(1, 4):
        in_copy(VOL, k).wait_recv()
    assemble(VOL)
    halo_start(VOL)

    for k in range(1, 4):
        w_copy(k).wait_recv()

    def taps_of(which):
        parts = [w_got[s, which].astype(F32) for s in range(4)]
        groups = [
            jnp.concatenate([part[8 * a : 8 * a + 8] for part in parts], axis=0) for a in range(7)
        ]

        def tap(dx, dy, dz):
            t = (dx * 3 + dy) * 3 + dz
            return groups[t // 4][:, 32 * (t % 4) : 32 * (t % 4) + 32]

        return groups, tap

    def make_forward(which):
        groups, tap = taps_of(which)
        for dz in range(3):
            line = jnp.concatenate([tap(k // 3, k % 3, dz) for k in range(9)], axis=1)
            lhs[2 * which, 32 * dz : 32 * dz + 32] = line.astype(BF16)
        return groups

    def make_turned(which):
        _, tap = taps_of(which)
        zeros = jnp.zeros((32, 32), F32)
        for dx in range(3):
            lines = [
                jnp.concatenate([tap(2 - dx, 2 - dy, 2 - dz) for dz in range(3)] + [zeros], axis=1)
                for dy in range(3)
            ]
            lines.append(jnp.zeros((32, 128), F32))
            block = jnp.concatenate(lines, axis=0)
            lhs[2 * which + 1, :, 96 * dx : 96 * dx + 96] = block.T[:96, :96].astype(BF16)

    groups = make_forward(0)
    bias_all = groups[6][:, 96:97] + groups[6][:, 97:98] + groups[6][:, 98:99]
    make_turned(1)

    lane = iota((32, 128), 1)
    not_first = lane > 0
    not_last = lane < 127

    def shift_up(rows):
        return jnp.where(not_first, pltpu.roll(rows, 1, 1), 0.0)

    def shift_down(rows):
        return jnp.where(not_last, pltpu.roll(rows, 127, 1), 0.0)

    def window(which, x, dx):
        return jnp.concatenate(
            [field[which, x + dx, y : y + 3].reshape(96, 128) for y in range(4)], axis=1
        )

    def conv(which, number, x):
        block = jnp.concatenate([window(which, x, dx) for dx in range(3)], axis=0)
        sums = jnp.dot(lhs[number], block, preferred_element_type=F32)
        lines = []
        for y in range(4):
            part = sums[:, 128 * y : 128 * y + 128]
            lines.append(part[32:64] + shift_up(part[0:32]) + shift_down(part[64:96]))
        return lines

    halo_wait(VOL)
    for x in range(4):
        for y, line in enumerate(conv(VOL, 0, x)):
            act = line + bias_all
            pre_act[x, y] = act
            field[HID, 1 + x, 1 + y] = (act / (1.0 + jnp.exp(-act))).astype(BF16)
    halo_start(HID)

    for k in range(1, 4):
        in_copy(COT, k).wait_recv()
    assemble(COT)
    halo_start(COT)
    make_forward(1)
    make_turned(0)
    halo_wait(COT)
    bias_sum = jnp.zeros((32, 128), F32)
    for x in range(4):
        for y, line in enumerate(conv(COT, 3, x)):
            act = pre_act[x, y]
            sig = 1.0 / (1.0 + jnp.exp(-act))
            value = (line * sig * (1.0 + act * (1.0 - sig))).astype(BF16)
            bias_sum = bias_sum + value.astype(F32)
            field[PRE, 1 + x, 1 + y] = value
    halo_start(PRE)

    def shifted(which, x, flip):
        columns = []
        for y in range(4):
            rows = field[which, 1 + x, 1 + y].astype(F32)
            up, down = shift_up(rows), shift_down(rows)
            trio = [down, rows, up] if flip else [up, rows, down]
            columns.append(jnp.concatenate(trio, axis=0).astype(BF16))
        return jnp.concatenate(columns, axis=1)

    along = (((1,), (1,)), ((), ()))

    acc_one = [jnp.zeros((96, 96), F32) for _ in range(3)]
    acc_two = [jnp.zeros((96, 96), F32) for _ in range(3)]
    for x in range(4):
        own_pre = shifted(PRE, x, True)
        own_hid = shifted(HID, x, False)
        for dx in range(3):
            acc_one[dx] = acc_one[dx] + lax.dot_general(
                own_pre, window(VOL, x, dx), along, preferred_element_type=F32
            )
            acc_two[dx] = acc_two[dx] + lax.dot_general(
                window(COT, x, dx), own_hid, along, preferred_element_type=F32
            )
    bias_own = jnp.sum(bias_sum, axis=1, keepdims=True)
    for dx in range(3):
        for k in range(3):
            for s in range(4):
                rows = slice(32 * k + 8 * s, 32 * k + 8 * s + 8)
                grad[0, s, 3 * dx + k, :, 0:96] = acc_one[dx][rows]
                grad[1, s, 3 * dx + k, :, 0:96] = acc_two[dx][rows]
    for s in range(4):
        grad[0, s, 0, :, 96:97] = bias_own[8 * s : 8 * s + 8]

    core_copy = pltpu.make_async_remote_copy(
        src_ref=grad.at[1 - core],
        dst_ref=core_got,
        send_sem=core_send.at[0],
        recv_sem=core_recv.at[0],
        device_id={"gx": 2 * row + 1 - core},
        device_id_type=MESH,
    )
    core_copy.start()

    def out_copy(which, k):
        return pltpu.make_async_remote_copy(
            src_ref=out_stage.at[which, af_peer[k]],
            dst_ref=out_got.at[which, sub],
            send_sem=out_send.at[which, k],
            recv_sem=out_recv.at[which, k],
            device_id={"af": af_peer[k]},
            device_id_type=MESH,
        )

    def produce(which, source, number):
        for x in range(4):
            lines = conv(source, number, x)
            for pair in range(2):
                for s in range(4):
                    rows = [lines[2 * pair + odd][8 * s : 8 * s + 8] for odd in range(2)]
                    out_stage[which, s, x, pair] = jnp.concatenate(rows, axis=0).astype(BF16)
        out_got[which, pl.ds(sub, 1)] = out_stage[which, pl.ds(af, 1)]
        for k in (2, 1, 3):
            out_copy(which, k).start()

    halo_wait(HID)
    produce(0, HID, 2)

    core_copy.wait_recv()
    core_sum[...] = grad[core] + core_got[...]
    z_got[af] = core_sum[af]

    def z_copy(k):
        return pltpu.make_async_remote_copy(
            src_ref=core_sum.at[af_peer[k]],
            dst_ref=z_got.at[af],
            send_sem=z_send.at[k],
            recv_sem=z_recv.at[k],
            device_id={"af": af_peer[k]},
            device_id_type=MESH,
        )

    for k in range(1, 4):
        z_copy(k).start()

    halo_wait(PRE)
    produce(1, PRE, 1)

    for k in range(1, 4):
        z_copy(k).wait_recv()
    y_got[row] = z_got[0] + z_got[1] + z_got[2] + z_got[3]

    def y_copy(k):
        return pltpu.make_async_remote_copy(
            src_ref=y_got.at[row],
            dst_ref=y_got.at[row],
            send_sem=y_send.at[k],
            recv_sem=y_recv.at[k],
            device_id={"gx": 2 * ((row + k) % n_y) + core},
            device_id_type=MESH,
        )

    for k in range(1, n_y):
        y_copy(k).start()
    for k in range(1, n_y):
        y_copy(k).wait_recv()
    x_got[col] = sum([y_got[i] for i in range(1, n_y)], y_got[0])

    def x_copy(k):
        return pltpu.make_async_remote_copy(
            src_ref=x_got.at[col],
            dst_ref=x_got.at[col],
            send_sem=x_send.at[k],
            recv_sem=x_recv.at[k],
            device_id={"gy": high * n_x + (col + k) % n_x},
            device_id_type=MESH,
        )

    for k in range(1, n_x):
        x_copy(k).start()
    for k in range(1, n_x):
        x_copy(k).wait_recv()
    h_stage[...] = sum([x_got[i] for i in range(1, n_x)], x_got[0])
    h_copy = pltpu.make_async_remote_copy(
        src_ref=h_stage,
        dst_ref=h_got,
        send_sem=h_send.at[0],
        recv_sem=h_recv.at[0],
        device_id={"gy": (1 - high) * n_x + col},
        device_id_type=MESH,
    )
    h_copy.start()

    def finish(which, target):
        for k in range(1, 4):
            out_copy(which, k).wait_recv()
        block = jnp.concatenate(
            [
                jnp.concatenate([out_got[which, j, x].reshape(32, 128) for j in range(4)], axis=0)
                for x in range(4)
            ],
            axis=1,
        )
        moved = jnp.dot(from_wire, block, preferred_element_type=F32).astype(BF16)
        for x in range(4):
            target[:, x] = moved[:, 128 * x : 128 * x + 128].reshape(8, 16, 128)

    finish(0, out)
    stores[0].start()
    h_copy.wait_recv()
    scale = 1.0 / math.sqrt(4 * n_gx * 16 * n_gy * 128)
    final[core] = (h_stage[...] + h_got[...]) * scale
    last_copy = pltpu.make_async_remote_copy(
        src_ref=final.at[core],
        dst_ref=final.at[core],
        send_sem=core_send.at[1],
        recv_sem=core_recv.at[1],
        device_id={"gx": 2 * row + 1 - core},
        device_id_type=MESH,
    )
    last_copy.start()
    finish(1, in_grad)
    stores[1].start()
    last_copy.wait_recv()
    for dx in range(3):
        for k in range(3):
            tile_one = final[0, 3 * dx + k]
            tile_two = final[1, 3 * dx + k]
            for m in range(3):
                g_one[dx, m, k] = tile_one[:, 32 * m : 32 * m + 32]
                g_two[2 - dx, 2 - k, m] = tile_two[:, 32 * m : 32 * m + 32]
    g_bias[...] = jnp.sum(jnp.where(diag, final[0, 0][:, 96:97], 0.0), axis=0, keepdims=True)
    for copy in stores[2:]:
        copy.start()

    for k in range(1, 4):
        in_copy(VOL, k).wait_send()
        in_copy(COT, k).wait_send()
        w_copy(k).wait_send()
        out_copy(0, k).wait_send()
        out_copy(1, k).wait_send()
        z_copy(k).wait_send()
    for which in (VOL, COT, HID, PRE):
        for side in SIDES:

            @pl.when(has(*side))
            def _(which=which, side=side):
                halo_copy(which, side).wait_send()

    core_copy.wait_send()
    for k in range(1, n_y):
        y_copy(k).wait_send()
    for k in range(1, n_x):
        x_copy(k).wait_send()
    h_copy.wait_send()
    last_copy.wait_send()
    for copy in stores:
        copy.wait()


def store(*refs):
    sources, targets, sems = refs[:5], refs[5:10], refs[10]
    copies = [
        pltpu.make_async_copy(source, target, sems.at[i])
        for i, (source, target) in enumerate(zip(sources, targets))
    ]
    for copy in copies:
        copy.start()
    for copy in copies:
        copy.wait()


def body(dims, volume, weight_one, bias_one, weight_two, cotangent):
    n_y, n_x = dims[0] // 2, dims[1] // 2
    as_taps = (2, 3, 4, 0, 1)
    dma = pltpu.SemaphoreType.DMA
    out, in_grad, g_one, g_bias, g_two = pl.pallas_call(
        functools.partial(kernel, dims),
        out_shape=(
            jax.ShapeDtypeStruct((8, 4, 16, 128), BF16),
            jax.ShapeDtypeStruct((8, 4, 16, 128), BF16),
            jax.ShapeDtypeStruct((3, 3, 3, 8, 32), F32),
            jax.ShapeDtypeStruct((1, 8), F32),
            jax.ShapeDtypeStruct((3, 3, 3, 8, 32), F32),
        ),
        in_specs=[pl.BlockSpec(memory_space=pltpu.HBM)] * 5,
        out_specs=[pl.BlockSpec(memory_space=pltpu.HBM)] * 5,
        scratch_shapes=[
            pltpu.VMEM((8, 4, 16, 128), BF16),
            pltpu.VMEM((8, 4, 16, 128), BF16),
            pltpu.VMEM((3, 3, 3, 8, 32), F32),
            pltpu.VMEM((1, 8), F32),
            pltpu.VMEM((3, 3, 3, 8, 32), F32),
            pltpu.VMEM((8, 4, 16, 128), BF16),
            pltpu.VMEM((3, 3, 3, 8, 32), BF16),
            pltpu.VMEM((1, 8), F32),
            pltpu.VMEM((3, 3, 3, 8, 32), BF16),
            pltpu.VMEM((8, 4, 16, 128), BF16),
            pltpu.VMEM((2, 4, 4, 2, 16, 128), BF16),
            pltpu.VMEM((2, 4, 4, 2, 16, 128), BF16),
            pltpu.VMEM((2, 64, 128), BF16),
            pltpu.VMEM((4, 2, 64, 128), BF16),
            pltpu.VMEM((4, 6, 6, 32, 128), BF16),
            pltpu.VMEM((4, 4, 32, 128), F32),
            pltpu.VMEM((4, 96, 288), BF16),
            pltpu.VMEM((2, 4, 4, 2, 16, 128), BF16),
            pltpu.VMEM((2, 4, 4, 2, 16, 128), BF16),
            pltpu.VMEM((2, 4, 9, 8, 128), F32),
            pltpu.VMEM((4, 9, 8, 128), F32),
            pltpu.VMEM((4, 9, 8, 128), F32),
            pltpu.VMEM((4, 9, 8, 128), F32),
            pltpu.VMEM((n_y, 9, 8, 128), F32),
            pltpu.VMEM((n_x, 9, 8, 128), F32),
            pltpu.VMEM((9, 8, 128), F32),
            pltpu.VMEM((9, 8, 128), F32),
            pltpu.VMEM((2, 9, 8, 128), F32),
            dma((2, 4)), dma((2, 4)), dma((4,)), dma((4,)), dma((4, 8)), dma((4, 8)), dma((2, 4)), dma((2, 4)),
            dma((2,)), dma((2,)), dma((4,)), dma((4,)), dma((4,)), dma((4,)), dma((4,)), dma((4,)), dma((1,)), dma((1,)),
            dma((5,)), dma((5,)),
        ],
        compiler_params=pltpu.CompilerParams(
            collective_id=0, has_side_effects=True, vmem_limit_bytes=60 * 1024 * 1024
        ),
    )(
        volume,
        jnp.transpose(weight_one, as_taps),
        bias_one.reshape(1, 8),
        jnp.transpose(weight_two, as_taps),
        cotangent,
    )
    results = (out, in_grad, g_one, g_bias, g_two)
    out, in_grad, g_one, g_bias, g_two = pl.pallas_call(
        store,
        out_shape=tuple(jax.ShapeDtypeStruct(part.shape, part.dtype) for part in results),
        in_specs=[pl.BlockSpec(memory_space=pltpu.HBM)] * 5,
        out_specs=[pl.BlockSpec(memory_space=pltpu.HBM)] * 5,
        scratch_shapes=[dma((5,))],
        compiler_params=pltpu.CompilerParams(vmem_limit_bytes=60 * 1024 * 1024),
    )(*results)
    as_given = (3, 4, 0, 1, 2)
    return (
        out,
        in_grad,
        jnp.transpose(g_one, as_given),
        g_bias.reshape(8),
        jnp.transpose(g_two, as_given),
    )


def solution(mesh):
    dims = (mesh.shape["gx"], mesh.shape["gy"])
    return jax.shard_map(
        functools.partial(body, dims),
        mesh=mesh,
        in_specs=(
            P("af", "gx", "gy", None),
            P("af", None, None, None, None),
            P("af"),
            P("af", None, None, None, None),
            P("af", "gx", "gy", None),
        ),
        out_specs=(
            P("af", "gx", "gy", None),
            P("af", "gx", "gy", None),
            P("af", None, None, None, None),
            P("af"),
            P("af", None, None, None, None),
        ),
        check_vma=False,
    )
```

```python
import functools
import math

import jax
import jax.numpy as jnp
from jax import lax
from jax.experimental import pallas as pl
from jax.experimental.pallas import tpu as pltpu
from jax.sharding import PartitionSpec as P

MESH = pl.DeviceIdType.MESH
F32 = jnp.float32
BF16 = jnp.bfloat16

VOL, COT, HID, PRE = 0, 1, 2, 3
SIDES = [(dx, dy) for dx in (-1, 0, 1) for dy in (-1, 0, 1) if (dx, dy) != (0, 0)]
SEND = {-1: (1, 1), 0: (1, 4), 1: (4, 1)}
EDGE = {-1: (0, 1), 0: (1, 4), 1: (5, 1)}
LAND = {-1: (5, 1), 0: (1, 4), 1: (0, 1)}


def iota(shape, dim):
    return lax.broadcasted_iota(jnp.int32, shape, dim)


def kernel(
    dims,
    vol_in, w_one_in, bias_in, w_two_in, cot_in,
    out_to, in_grad_to, g_one_to, g_bias_to, g_two_to,
    out, in_grad, g_one, g_bias, g_two,
    vol, w_one, bias, w_two, cot,
    stage, got, w_stage, w_got, field, pre_act, lhs,
    out_stage, out_got, grad, core_got, core_sum, plane_got, line_stage, line_got, final,
    in_send, in_recv, w_send, w_recv, pass_send, pass_recv, halo_send, halo_recv, out_send, out_recv,
    core_send, core_recv, plane_send, plane_recv, line_send, line_recv, last_send, last_recv, load_sem, store_sem,
):
    loads = [
        pltpu.make_async_copy(source, target, load_sem.at[i])
        for i, (source, target) in enumerate(
            ((vol_in, vol), (w_one_in, w_one), (w_two_in, w_two), (bias_in, bias), (cot_in, cot))
        )
    ]
    for load in loads:
        load.start()
    stores = [
        pltpu.make_async_copy(source, target, store_sem.at[i])
        for i, (source, target) in enumerate(
            ((out, out_to), (in_grad, in_grad_to), (g_one, g_one_to), (g_bias, g_bias_to), (g_two, g_two_to))
        )
    ]
    n_gx, n_gy = dims
    n_y, n_x = n_gx // 2, n_gy // 2
    gx, gy, af = lax.axis_index("gx"), lax.axis_index("gy"), lax.axis_index("af")
    row, core = gx // 2, gx % 2
    col, high = gy % n_x, gy // n_x

    def turned(at):
        even = (at % 2) == 0
        upper = at >= n_x
        return jnp.logical_xor(even, upper)

    def sub_of(at_af, at_gy):
        return jnp.where(turned(at_gy), 3 - at_af, at_af)

    sub = sub_of(af, gy)

    def y_neighbour(step):
        if step == 0:
            return gy, af
        inside = (sub < 3) if step > 0 else (sub > 0)
        gy_new = jnp.where(inside, gy, gy + step)
        sub_new = jnp.where(inside, sub + step, 0 if step > 0 else 3)
        return gy_new, sub_of(sub_new, gy_new)

    def has(dx, dy):
        checks = []
        if dx < 0:
            checks.append(gx > 0)
        if dx > 0:
            checks.append(gx < n_gx - 1)
        if dy < 0:
            checks.append(jnp.logical_or(gy > 0, sub > 0))
        if dy > 0:
            checks.append(jnp.logical_or(gy < n_gy - 1, sub < 3))
        if len(checks) == 1:
            return checks[0]
        return jnp.logical_and(checks[0], checks[1])

    neighbour = {}
    for dx, dy in SIDES:
        gy_new, af_new = y_neighbour(dy)
        neighbour[dx, dy] = {"gx": gx + dx, "gy": gy_new, "af": af_new}
    af_peer = [(af + k) % 4 for k in range(4)]

    plane = n_y * n_x
    place = row * n_x + col
    kept = 16 // plane

    def at_place(k):
        other = (place + k) % plane
        return other // n_x, high * n_x + other % n_x

    barrier = pltpu.get_barrier_semaphore()
    partners = []
    for k in range(plane):
        other_row, other_gy = at_place(k)
        for other_core in (1 - core, core):
            partners.append({"gx": 2 * other_row + other_core, "gy": other_gy, "af": af})
    partners.pop(1)
    for k in range(1, 8):
        partners.append({"gx": gx, "gy": ((high + k // 4) % 2) * n_x + col, "af": af_peer[k % 4]})
    for partner in partners:
        pl.semaphore_signal(barrier, inc=1, device_id=partner, device_id_type=MESH)
    expected = jnp.int32(len(partners))
    for side in SIDES:

        @pl.when(has(*side))
        def _(side=side):
            pl.semaphore_signal(barrier, inc=1, device_id=neighbour[side], device_id_type=MESH)

        expected = expected + has(*side).astype(jnp.int32)

        @pl.when(jnp.logical_not(has(*side)))
        def _(side=side):
            (fx, cx), (fy, cy) = EDGE[side[0]], EDGE[side[1]]
            field[:, fx : fx + cx, fy : fy + cy] = jnp.zeros((4, cx, cy, 32, 128), BF16)

    r, q = iota((128, 128), 0), iota((128, 128), 1)
    to_wire = jnp.where(q == (r % 8) * 16 + r // 8, 1.0, 0.0).astype(BF16)
    from_wire = jnp.where(q == (r % 16) * 8 + r // 16, 1.0, 0.0).astype(BF16)

    def stage_input(which, source):
        block = jnp.concatenate([source[:, x].reshape(128, 128) for x in range(4)], axis=1)
        moved = jnp.dot(to_wire, block, preferred_element_type=F32).astype(BF16)
        for x in range(4):
            for j in range(4):
                part = moved[32 * j : 32 * j + 32, 128 * x : 128 * x + 128]
                stage[which, j, x] = part.reshape(2, 16, 128)
        got[which, pl.ds(af, 1)] = stage[which, pl.ds(sub, 1)]

    def in_copy(which, k):
        return pltpu.make_async_remote_copy(
            src_ref=stage.at[which, sub_of(af_peer[k], gy)],
            dst_ref=got.at[which, af],
            send_sem=in_send.at[which, k],
            recv_sem=in_recv.at[which, k],
            device_id={"af": af_peer[k]},
            device_id_type=MESH,
        )

    def w_copy(k):
        return pltpu.make_async_remote_copy(
            src_ref=w_stage.at[core],
            dst_ref=w_got.at[af, core],
            send_sem=w_send.at[k],
            recv_sem=w_recv.at[k],
            device_id={"af": af_peer[k]},
            device_id_type=MESH,
        )

    def pass_copy(k):
        origin = (af + 4 - k) % 4
        return pltpu.make_async_remote_copy(
            src_ref=w_got.at[origin, core],
            dst_ref=w_got.at[origin, core],
            send_sem=pass_send.at[k],
            recv_sem=pass_recv.at[k],
            device_id={"gx": 2 * row + 1 - core},
            device_id_type=MESH,
        )

    loads[0].wait()
    stage_input(VOL, vol)
    pl.semaphore_wait(barrier, expected)
    for k in (2, 1, 3):
        in_copy(VOL, k).start()

    for load in loads[1:]:
        load.wait()
    diag = iota((8, 8), 0) == iota((8, 8), 1)
    bias_col = jnp.sum(jnp.where(diag, bias[...], 0.0), axis=1, keepdims=True)
    part_a = bias_col.astype(BF16).astype(F32)
    part_b = (bias_col - part_a).astype(BF16).astype(F32)
    part_c = (bias_col - part_a) - part_b
    lane32 = iota((8, 32), 1)
    spare = jnp.where(lane32 == 0, part_a, jnp.where(lane32 == 1, part_b, jnp.where(lane32 == 2, part_c, 0.0)))
    for which, weight in enumerate((w_one, w_two)):
        groups = []
        for a in range(7):
            taps = []
            for b in range(4):
                t = 4 * a + b
                taps.append(weight[t // 9, (t // 3) % 3, t % 3].astype(F32) if t < 27 else spare)
            groups.append(jnp.concatenate(taps, axis=1))
        groups.append(jnp.zeros((8, 128), F32))
        packed = jnp.concatenate(groups, axis=0).astype(BF16)
        w_stage[which] = packed
        w_got[af, which] = packed
    for k in (2, 1, 3):
        w_copy(k).start()
    stage_input(COT, cot)
    for k in (2, 1, 3):
        in_copy(VOL, k).wait_send()
    for k in (2, 1, 3):
        in_copy(COT, k).start()

    def halo_copy(which, side):
        number = SIDES.index(side)
        (sx, nx), (sy, ny) = SEND[side[0]], SEND[side[1]]
        (lx, _), (ly, _) = LAND[side[0]], LAND[side[1]]
        return pltpu.make_async_remote_copy(
            src_ref=field.at[which, sx : sx + nx, sy : sy + ny],
            dst_ref=field.at[which, lx : lx + nx, ly : ly + ny],
            send_sem=halo_send.at[which, number],
            recv_sem=halo_recv.at[which, number],
            device_id=neighbour[side],
            device_id_type=MESH,
        )

    def halo_start(which):
        for side in SIDES:

            @pl.when(has(*side))
            def _(side=side):
                halo_copy(which, side).start()

    def halo_wait(which):
        for side in SIDES:

            @pl.when(has(-side[0], -side[1]))
            def _(side=side):
                halo_copy(which, side).wait_recv()

    def assemble(which):
        for x in range(4):
            for pair in range(2):
                parts = [got[which, s, x, pair].astype(F32) for s in range(4)]
                for odd in range(2):
                    rows = [part[8 * odd : 8 * odd + 8] for part in parts]
                    field[which, 1 + x, 1 + 2 * pair + odd] = jnp.concatenate(rows, axis=0).astype(BF16)

    for k in range(1, 4):
        in_copy(VOL, k).wait_recv()
    assemble(VOL)
    halo_start(VOL)

    for k in range(1, 4):
        w_copy(k).wait_recv()
        pass_copy(k).start()
    for k in range(1, 4):
        pass_copy(k).wait_recv()

    def taps_of(which):
        parts = [w_got[s, which].astype(F32) for s in range(4)]
        groups = [
            jnp.concatenate([part[8 * a : 8 * a + 8] for part in parts], axis=0) for a in range(7)
        ]

        def tap(dx, dy, dz):
            t = (dx * 3 + dy) * 3 + dz
            return groups[t // 4][:, 32 * (t % 4) : 32 * (t % 4) + 32]

        return groups, tap

    def make_forward(which):
        groups, tap = taps_of(which)
        for dz in range(3):
            line = jnp.concatenate([tap(k // 3, k % 3, dz) for k in range(9)], axis=1)
            lhs[2 * which, 32 * dz : 32 * dz + 32] = line.astype(BF16)
        return groups

    def make_turned(which):
        _, tap = taps_of(which)
        zeros = jnp.zeros((32, 32), F32)
        for dx in range(3):
            lines = [
                jnp.concatenate([tap(2 - dx, 2 - dy, 2 - dz) for dz in range(3)] + [zeros], axis=1)
                for dy in range(3)
            ]
            lines.append(jnp.zeros((32, 128), F32))
            block = jnp.concatenate(lines, axis=0)
            lhs[2 * which + 1, :, 96 * dx : 96 * dx + 96] = block.T[:96, :96].astype(BF16)

    groups = make_forward(0)
    bias_all = groups[6][:, 96:97] + groups[6][:, 97:98] + groups[6][:, 98:99]
    make_turned(1)

    lane = iota((32, 128), 1)
    not_first = lane > 0
    not_last = lane < 127

    def shift_up(rows):
        return jnp.where(not_first, pltpu.roll(rows, 1, 1), 0.0)

    def shift_down(rows):
        return jnp.where(not_last, pltpu.roll(rows, 127, 1), 0.0)

    def window(which, x, dx):
        return jnp.concatenate(
            [field[which, x + dx, y : y + 3].reshape(96, 128) for y in range(4)], axis=1
        )

    def conv(which, number, x):
        block = jnp.concatenate([window(which, x, dx) for dx in range(3)], axis=0)
        sums = jnp.dot(lhs[number], block, preferred_element_type=F32)
        lines = []
        for y in range(4):
            part = sums[:, 128 * y : 128 * y + 128]
            lines.append(part[32:64] + shift_up(part[0:32]) + shift_down(part[64:96]))
        return lines

    halo_wait(VOL)
    for x in range(4):
        for y, line in enumerate(conv(VOL, 0, x)):
            act = line + bias_all
            pre_act[x, y] = act
            field[HID, 1 + x, 1 + y] = (act / (1.0 + jnp.exp(-act))).astype(BF16)
    halo_start(HID)

    for k in range(1, 4):
        in_copy(COT, k).wait_recv()
    assemble(COT)
    halo_start(COT)
    make_forward(1)
    make_turned(0)
    halo_wait(COT)
    bias_sum = jnp.zeros((32, 128), F32)
    for x in range(4):
        for y, line in enumerate(conv(COT, 3, x)):
            act = pre_act[x, y]
            sig = 1.0 / (1.0 + jnp.exp(-act))
            value = (line * sig * (1.0 + act * (1.0 - sig))).astype(BF16)
            bias_sum = bias_sum + value.astype(F32)
            field[PRE, 1 + x, 1 + y] = value
    halo_start(PRE)

    def shifted(which, x, flip):
        columns = []
        for y in range(4):
            rows = field[which, 1 + x, 1 + y].astype(F32)
            up, down = shift_up(rows), shift_down(rows)
            trio = [down, rows, up] if flip else [up, rows, down]
            columns.append(jnp.concatenate(trio, axis=0).astype(BF16))
        return jnp.concatenate(columns, axis=1)

    along = (((1,), (1,)), ((), ()))

    acc_one = [jnp.zeros((96, 96), F32) for _ in range(3)]
    acc_two = [jnp.zeros((96, 96), F32) for _ in range(3)]
    for x in range(4):
        own_pre = shifted(PRE, x, True)
        own_hid = shifted(HID, x, False)
        for dx in range(3):
            acc_one[dx] = acc_one[dx] + lax.dot_general(
                own_pre, window(VOL, x, dx), along, preferred_element_type=F32
            )
            acc_two[dx] = acc_two[dx] + lax.dot_general(
                window(COT, x, dx), own_hid, along, preferred_element_type=F32
            )
    bias_own = jnp.sum(bias_sum, axis=1, keepdims=True)
    for which, acc in enumerate((acc_one, acc_two)):
        for s in range(4):
            blocks = [acc[k // 3][32 * (k % 3) + 8 * s : 32 * (k % 3) + 8 * s + 8] for k in range(9)]
            tiles = []
            for k in range(6):
                cut = blocks[6 + k // 3][:, 32 * (k % 3) : 32 * (k % 3) + 32]
                tiles.append(jnp.concatenate([blocks[k], cut], axis=1))
            if which == 0:
                extra = jnp.broadcast_to(bias_own[8 * s : 8 * s + 8], (8, 32))
            else:
                extra = jnp.zeros((8, 32), F32)
            tiles.append(jnp.concatenate([blocks[8], extra], axis=1))
            tiles.append(jnp.zeros((8, 128), F32))
            for k in range(8):
                grad[which, 4 * s + k // 2, k % 2] = tiles[k]

    core_copy = pltpu.make_async_remote_copy(
        src_ref=grad.at[1 - core],
        dst_ref=core_got,
        send_sem=core_send.at[0],
        recv_sem=core_recv.at[0],
        device_id={"gx": 2 * row + 1 - core},
        device_id_type=MESH,
    )
    core_copy.start()

    def out_copy(which, k):
        return pltpu.make_async_remote_copy(
            src_ref=out_stage.at[which, af_peer[k]],
            dst_ref=out_got.at[which, sub],
            send_sem=out_send.at[which, k],
            recv_sem=out_recv.at[which, k],
            device_id={"af": af_peer[k]},
            device_id_type=MESH,
        )

    def produce(which, source, number):
        for x in range(4):
            lines = conv(source, number, x)
            for pair in range(2):
                for s in range(4):
                    rows = [lines[2 * pair + odd][8 * s : 8 * s + 8] for odd in range(2)]
                    out_stage[which, s, x, pair] = jnp.concatenate(rows, axis=0).astype(BF16)
        out_got[which, pl.ds(sub, 1)] = out_stage[which, pl.ds(af, 1)]
        for k in (2, 1, 3):
            out_copy(which, k).start()

    halo_wait(HID)
    produce(0, HID, 2)

    core_copy.wait_recv()
    core_sum[...] = grad[core] + core_got[...]
    plane_got[place] = core_sum[pl.ds(place * kept, kept)]

    def plane_copy(k):
        other_row, other_gy = at_place(k)
        return pltpu.make_async_remote_copy(
            src_ref=core_sum.at[pl.ds(((place + k) % plane) * kept, kept)],
            dst_ref=plane_got.at[place],
            send_sem=plane_send.at[k],
            recv_sem=plane_recv.at[k],
            device_id={"gx": 2 * other_row + core, "gy": other_gy},
            device_id_type=MESH,
        )

    for k in range(1, plane):
        plane_copy(k).start()

    halo_wait(PRE)
    produce(1, PRE, 1)

    for k in range(1, plane):
        plane_copy(k).wait_recv()
    line_stage[...] = sum([plane_got[i] for i in range(1, plane)], plane_got[0])

    owner = (place * kept) // 4
    mine = af == owner
    at_line = high * 4 + af

    def line_copy(half):
        return pltpu.make_async_remote_copy(
            src_ref=line_stage,
            dst_ref=line_got.at[at_line],
            send_sem=line_send.at[half],
            recv_sem=line_recv.at[at_line],
            device_id={"gy": half * n_x + col, "af": owner},
            device_id_type=MESH,
        )

    def not_here(half):
        return jnp.logical_not(jnp.logical_and(mine, high == half))

    for half in range(2):

        @pl.when(not_here(half))
        def _(half=half):
            line_copy(half).start()

    @pl.when(mine)
    def _():
        line_got[at_line] = line_stage[...]

    def finish(which, target):
        for k in range(1, 4):
            out_copy(which, k).wait_recv()
        block = jnp.concatenate(
            [
                jnp.concatenate([out_got[which, j, x].reshape(32, 128) for j in range(4)], axis=0)
                for x in range(4)
            ],
            axis=1,
        )
        moved = jnp.dot(from_wire, block, preferred_element_type=F32).astype(BF16)
        for x in range(4):
            target[:, x] = moved[:, 128 * x : 128 * x + 128].reshape(8, 16, 128)

    finish(0, out)
    stores[0].start()
    scale = 1.0 / math.sqrt(4 * n_gx * 16 * n_gy * 128)
    quarter = (place * kept) % 4

    def last_copy(k, same):
        other_row, other_gy = at_place(k)
        return pltpu.make_async_remote_copy(
            src_ref=final.at[core, pl.ds(quarter, kept)],
            dst_ref=final.at[core, pl.ds(quarter, kept)],
            send_sem=last_send.at[2 * k + same],
            recv_sem=last_recv.at[core, quarter],
            device_id={"gx": 2 * other_row + (core if same else 1 - core), "gy": other_gy},
            device_id_type=MESH,
        )

    @pl.when(mine)
    def _():
        for i in range(8):

            @pl.when(at_line != i)
            def _(i=i):
                pltpu.make_async_remote_copy(
                    src_ref=line_stage,
                    dst_ref=line_got.at[i],
                    send_sem=line_send.at[0],
                    recv_sem=line_recv.at[i],
                    device_id={"af": af_peer[1]},
                    device_id_type=MESH,
                ).wait_recv()

        total = sum([line_got[i] for i in range(1, 8)], line_got[0])
        final[core, pl.ds(quarter, kept)] = total * scale
        for k in range(plane):
            for same in (0, 1):
                if k > 0 or same == 0:
                    last_copy(k, same).start()

    finish(1, in_grad)
    stores[1].start()

    for kind in range(2):
        for part in range(0, 4, min(kept, 4)):

            @pl.when(jnp.logical_not(jnp.logical_and(mine, jnp.logical_and(core == kind, quarter == part))))
            def _(kind=kind, part=part):
                pltpu.make_async_remote_copy(
                    src_ref=final.at[kind, pl.ds(part, kept)],
                    dst_ref=final.at[kind, pl.ds(part, kept)],
                    send_sem=last_send.at[0],
                    recv_sem=last_recv.at[kind, part],
                    device_id={"gx": 2 * row + 1 - core},
                    device_id_type=MESH,
                ).wait_recv()

    for kind in range(2):
        tiles = [final[kind, k // 2, k % 2] for k in range(7)]
        for a in range(3):
            for b in range(3):
                for c in range(3):
                    k = 3 * a + b
                    if k < 6:
                        tap = tiles[k][:, 32 * c : 32 * c + 32]
                    elif k < 8:
                        tap = tiles[3 * (k - 6) + c][:, 96:128]
                    else:
                        tap = tiles[6][:, 32 * c : 32 * c + 32]
                    if kind == 0:
                        g_one[a, c, b] = tap
                    else:
                        g_two[2 - a, 2 - b, c] = tap
    g_bias[...] = jnp.sum(jnp.where(diag, final[0, 3, 0][:, 96:97], 0.0), axis=0, keepdims=True)
    for copy in stores[2:]:
        copy.start()

    for k in range(1, 4):
        in_copy(COT, k).wait_send()
        w_copy(k).wait_send()
        out_copy(0, k).wait_send()
        out_copy(1, k).wait_send()
        pass_copy(k).wait_send()
    for which in (VOL, COT, HID, PRE):
        for side in SIDES:

            @pl.when(has(*side))
            def _(which=which, side=side):
                halo_copy(which, side).wait_send()

    core_copy.wait_send()
    for k in range(1, plane):
        plane_copy(k).wait_send()
    for half in range(2):

        @pl.when(not_here(half))
        def _(half=half):
            line_copy(half).wait_send()

    @pl.when(mine)
    def _():
        for k in range(plane):
            for same in (0, 1):
                if k > 0 or same == 0:
                    last_copy(k, same).wait_send()

    for copy in stores:
        copy.wait()


def store(*refs):
    sources, targets, held, sems = refs[:5], refs[5:10], refs[10:15], refs[15]
    loads = [pltpu.make_async_copy(sources[i], held[i], sems.at[0, i]) for i in range(5)]
    copies = [pltpu.make_async_copy(held[i], targets[i], sems.at[1, i]) for i in range(5)]
    for load in loads:
        load.start()
    for load, copy in zip(loads, copies):
        load.wait()
        copy.start()
    for copy in copies:
        copy.wait()


def body(dims, volume, weight_one, bias_one, weight_two, cotangent):
    plane = (dims[0] // 2) * (dims[1] // 2)
    as_taps = (2, 3, 4, 0, 1)
    dma = pltpu.SemaphoreType.DMA
    out, in_grad, g_one, g_bias, g_two = pl.pallas_call(
        functools.partial(kernel, dims),
        out_shape=(
            jax.ShapeDtypeStruct((8, 4, 16, 128), BF16),
            jax.ShapeDtypeStruct((8, 4, 16, 128), BF16),
            jax.ShapeDtypeStruct((3, 3, 3, 8, 32), F32),
            jax.ShapeDtypeStruct((1, 8), F32),
            jax.ShapeDtypeStruct((3, 3, 3, 8, 32), F32),
        ),
        in_specs=[pl.BlockSpec(memory_space=pltpu.HBM)] * 5,
        out_specs=[pl.BlockSpec(memory_space=pltpu.HBM)] * 5,
        scratch_shapes=[
            pltpu.VMEM((8, 4, 16, 128), BF16),
            pltpu.VMEM((8, 4, 16, 128), BF16),
            pltpu.VMEM((3, 3, 3, 8, 32), F32),
            pltpu.VMEM((1, 8), F32),
            pltpu.VMEM((3, 3, 3, 8, 32), F32),
            pltpu.VMEM((8, 4, 16, 128), BF16),
            pltpu.VMEM((3, 3, 3, 8, 32), BF16),
            pltpu.VMEM((1, 8), F32),
            pltpu.VMEM((3, 3, 3, 8, 32), BF16),
            pltpu.VMEM((8, 4, 16, 128), BF16),
            pltpu.VMEM((2, 4, 4, 2, 16, 128), BF16),
            pltpu.VMEM((2, 4, 4, 2, 16, 128), BF16),
            pltpu.VMEM((2, 64, 128), BF16),
            pltpu.VMEM((4, 2, 64, 128), BF16),
            pltpu.VMEM((4, 6, 6, 32, 128), BF16),
            pltpu.VMEM((4, 4, 32, 128), F32),
            pltpu.VMEM((4, 96, 288), BF16),
            pltpu.VMEM((2, 4, 4, 2, 16, 128), BF16),
            pltpu.VMEM((2, 4, 4, 2, 16, 128), BF16),
            pltpu.VMEM((2, 16, 2, 8, 128), F32),
            pltpu.VMEM((16, 2, 8, 128), F32),
            pltpu.VMEM((16, 2, 8, 128), F32),
            pltpu.VMEM((plane, 16 // plane, 2, 8, 128), F32),
            pltpu.VMEM((16 // plane, 2, 8, 128), F32),
            pltpu.VMEM((8, 16 // plane, 2, 8, 128), F32),
            pltpu.VMEM((2, 4, 2, 8, 128), F32),
            dma((2, 4)), dma((2, 4)), dma((4,)), dma((4,)), dma((4,)), dma((4,)),
            dma((4, 8)), dma((4, 8)), dma((2, 4)), dma((2, 4)),
            dma((1,)), dma((1,)), dma((plane,)), dma((plane,)), dma((2,)), dma((8,)), dma((2 * plane,)), dma((2, 4)),
            dma((5,)), dma((5,)),
        ],
        compiler_params=pltpu.CompilerParams(
            collective_id=0, has_side_effects=True, vmem_limit_bytes=60 * 1024 * 1024
        ),
    )(
        volume,
        jnp.transpose(weight_one, as_taps),
        bias_one.reshape(1, 8),
        jnp.transpose(weight_two, as_taps),
        cotangent,
    )
    results = (out, in_grad, g_one, g_bias, g_two)
    out, in_grad, g_one, g_bias, g_two = pl.pallas_call(
        store,
        out_shape=tuple(jax.ShapeDtypeStruct(part.shape, part.dtype) for part in results),
        in_specs=[pl.BlockSpec(memory_space=pltpu.HBM)] * 5,
        out_specs=[pl.BlockSpec(memory_space=pltpu.HBM)] * 5,
        scratch_shapes=[pltpu.VMEM(part.shape, part.dtype) for part in results] + [dma((2, 5))],
        compiler_params=pltpu.CompilerParams(vmem_limit_bytes=60 * 1024 * 1024),
    )(*results)
    as_given = (3, 4, 0, 1, 2)
    return (
        out,
        in_grad,
        jnp.transpose(g_one, as_given),
        g_bias.reshape(8),
        jnp.transpose(g_two, as_given),
    )


def solution(mesh):
    dims = (mesh.shape["gx"], mesh.shape["gy"])
    return jax.shard_map(
        functools.partial(body, dims),
        mesh=mesh,
        in_specs=(
            P("af", "gx", "gy", None),
            P("af", None, None, None, None),
            P("af"),
            P("af", None, None, None, None),
            P("af", "gx", "gy", None),
        ),
        out_specs=(
            P("af", "gx", "gy", None),
            P("af", "gx", "gy", None),
            P("af", None, None, None, None),
            P("af"),
            P("af", None, None, None, None),
        ),
        check_vma=False,
    )
```

```python
import functools
import math

import jax
import jax.numpy as jnp
from jax import lax
from jax.experimental import pallas as pl
from jax.experimental.pallas import tpu as pltpu
from jax.sharding import PartitionSpec as P

MESH = pl.DeviceIdType.MESH
F32 = jnp.float32
BF16 = jnp.bfloat16

VOL, COT, HID, PRE = 0, 1, 2, 3
SIDES = [(dx, dy) for dx in (-1, 0, 1) for dy in (-1, 0, 1) if (dx, dy) != (0, 0)]
SEND = {-1: (1, 1), 0: (1, 4), 1: (4, 1)}
EDGE = {-1: (0, 1), 0: (1, 4), 1: (5, 1)}
LAND = {-1: (5, 1), 0: (1, 4), 1: (0, 1)}


def iota(shape, dim):
    return lax.broadcasted_iota(jnp.int32, shape, dim)


def kernel(
    dims,
    vol_in, w_one_in, bias_in, w_two_in, cot_in,
    out_to, in_grad_to, g_one_to, g_bias_to, g_two_to,
    out, in_grad, g_one, g_bias, g_two,
    vol, w_one, bias, w_two, cot,
    stage, got, w_stage, w_got, field, pre_act, lhs,
    out_stage, out_got, grad, core_got, core_sum, plane_got, line_stage, line_got, final,
    in_send, in_recv, w_send, w_recv, pass_send, pass_recv, halo_send, halo_recv, out_send, out_recv,
    core_send, core_recv, plane_send, plane_recv, line_send, line_recv, last_send, last_recv, load_sem, store_sem, line_in,
):
    loads = [
        pltpu.make_async_copy(source, target, load_sem.at[i])
        for i, (source, target) in enumerate(
            ((vol_in, vol), (w_one_in, w_one), (w_two_in, w_two), (bias_in, bias), (cot_in, cot))
        )
    ]
    for load in loads:
        load.start()
    stores = [
        pltpu.make_async_copy(source, target, store_sem.at[i])
        for i, (source, target) in enumerate(
            ((out, out_to), (in_grad, in_grad_to), (g_one, g_one_to), (g_bias, g_bias_to), (g_two, g_two_to))
        )
    ]
    n_gx, n_gy = dims
    n_y, n_x = n_gx // 2, n_gy // 2
    gx, gy, af = lax.axis_index("gx"), lax.axis_index("gy"), lax.axis_index("af")
    row, core = gx // 2, gx % 2
    col, high = gy % n_x, gy // n_x

    def turned(at):
        even = (at % 2) == 0
        upper = at >= n_x
        return jnp.logical_xor(even, upper)

    def sub_of(at_af, at_gy):
        return jnp.where(turned(at_gy), 3 - at_af, at_af)

    sub = sub_of(af, gy)

    def y_neighbour(step):
        if step == 0:
            return gy, af
        inside = (sub < 3) if step > 0 else (sub > 0)
        gy_new = jnp.where(inside, gy, gy + step)
        sub_new = jnp.where(inside, sub + step, 0 if step > 0 else 3)
        return gy_new, sub_of(sub_new, gy_new)

    def has(dx, dy):
        checks = []
        if dx < 0:
            checks.append(gx > 0)
        if dx > 0:
            checks.append(gx < n_gx - 1)
        if dy < 0:
            checks.append(jnp.logical_or(gy > 0, sub > 0))
        if dy > 0:
            checks.append(jnp.logical_or(gy < n_gy - 1, sub < 3))
        if len(checks) == 1:
            return checks[0]
        return jnp.logical_and(checks[0], checks[1])

    neighbour = {}
    for dx, dy in SIDES:
        gy_new, af_new = y_neighbour(dy)
        neighbour[dx, dy] = {"gx": gx + dx, "gy": gy_new, "af": af_new}
    af_peer = [(af + k) % 4 for k in range(4)]

    plane = n_y * n_x
    place = row * n_x + col
    kept = 16 // plane

    def at_place(k):
        other = (place + k) % plane
        return other // n_x, high * n_x + other % n_x

    barrier = pltpu.get_barrier_semaphore()
    across = [{"gy": high * n_x + (col + k) % n_x} for k in range(1, n_x)]
    across += [{"gy": (1 - high) * n_x + col}]
    partners = across + [{"af": af_peer[k]} for k in range(1, 4)]
    partners += [{"gx": 2 * ((row + k) % n_y) + core} for k in range(1, n_y)]
    for partner in partners:
        pl.semaphore_signal(barrier, inc=1, device_id=partner, device_id_type=MESH)
    expected = jnp.int32(len(partners))
    for side in SIDES:

        @pl.when(has(*side))
        def _(side=side):
            pl.semaphore_signal(barrier, inc=1, device_id=neighbour[side], device_id_type=MESH)

        expected = expected + has(*side).astype(jnp.int32)

        @pl.when(jnp.logical_not(has(*side)))
        def _(side=side):
            (fx, cx), (fy, cy) = EDGE[side[0]], EDGE[side[1]]
            field[:, fx : fx + cx, fy : fy + cy] = jnp.zeros((4, cx, cy, 32, 128), BF16)

    r, q = iota((128, 128), 0), iota((128, 128), 1)
    to_wire = jnp.where(q == (r % 8) * 16 + r // 8, 1.0, 0.0).astype(BF16)
    from_wire = jnp.where(q == (r % 16) * 8 + r // 16, 1.0, 0.0).astype(BF16)

    def stage_input(which, source):
        block = jnp.concatenate([source[:, x].reshape(128, 128) for x in range(4)], axis=1)
        moved = jnp.dot(to_wire, block, preferred_element_type=F32).astype(BF16)
        for x in range(4):
            for j in range(4):
                part = moved[32 * j : 32 * j + 32, 128 * x : 128 * x + 128]
                stage[which, j, x] = part.reshape(2, 16, 128)
        got[which, pl.ds(af, 1)] = stage[which, pl.ds(sub, 1)]

    def in_copy(which, k):
        return pltpu.make_async_remote_copy(
            src_ref=stage.at[which, sub_of(af_peer[k], gy)],
            dst_ref=got.at[which, af],
            send_sem=in_send.at[which, k],
            recv_sem=in_recv.at[which, k],
            device_id={"af": af_peer[k]},
            device_id_type=MESH,
        )

    def w_copy(k):
        return pltpu.make_async_remote_copy(
            src_ref=w_stage.at[core],
            dst_ref=w_got.at[af, core],
            send_sem=w_send.at[k],
            recv_sem=w_recv.at[k],
            device_id={"af": af_peer[k]},
            device_id_type=MESH,
        )

    def pass_copy(k):
        origin = (af + 4 - k) % 4
        return pltpu.make_async_remote_copy(
            src_ref=w_got.at[origin, core],
            dst_ref=w_got.at[origin, core],
            send_sem=pass_send.at[k],
            recv_sem=pass_recv.at[k],
            device_id={"gx": 2 * row + 1 - core},
            device_id_type=MESH,
        )

    loads[0].wait()
    stage_input(VOL, vol)
    pl.semaphore_wait(barrier, expected)
    for k in (2, 1, 3):
        in_copy(VOL, k).start()
    for partner in across:
        pl.semaphore_signal(line_in, inc=1, device_id=partner, device_id_type=MESH)

    for load in loads[1:]:
        load.wait()
    diag = iota((8, 8), 0) == iota((8, 8), 1)
    bias_col = jnp.sum(jnp.where(diag, bias[...], 0.0), axis=1, keepdims=True)
    part_a = bias_col.astype(BF16).astype(F32)
    part_b = (bias_col - part_a).astype(BF16).astype(F32)
    part_c = (bias_col - part_a) - part_b
    lane32 = iota((8, 32), 1)
    spare = jnp.where(lane32 == 0, part_a, jnp.where(lane32 == 1, part_b, jnp.where(lane32 == 2, part_c, 0.0)))
    for which, weight in enumerate((w_one, w_two)):
        groups = []
        for a in range(7):
            taps = []
            for b in range(4):
                t = 4 * a + b
                taps.append(weight[t // 9, (t // 3) % 3, t % 3].astype(F32) if t < 27 else spare)
            groups.append(jnp.concatenate(taps, axis=1))
        groups.append(jnp.zeros((8, 128), F32))
        packed = jnp.concatenate(groups, axis=0).astype(BF16)
        w_stage[which] = packed
        w_got[af, which] = packed
    for k in (2, 1, 3):
        w_copy(k).start()
    stage_input(COT, cot)
    for k in (2, 1, 3):
        in_copy(VOL, k).wait_send()
    for k in (2, 1, 3):
        in_copy(COT, k).start()

    def halo_copy(which, side):
        number = SIDES.index(side)
        (sx, nx), (sy, ny) = SEND[side[0]], SEND[side[1]]
        (lx, _), (ly, _) = LAND[side[0]], LAND[side[1]]
        return pltpu.make_async_remote_copy(
            src_ref=field.at[which, sx : sx + nx, sy : sy + ny],
            dst_ref=field.at[which, lx : lx + nx, ly : ly + ny],
            send_sem=halo_send.at[which, number],
            recv_sem=halo_recv.at[which, number],
            device_id=neighbour[side],
            device_id_type=MESH,
        )

    def halo_start(which):
        for side in SIDES:

            @pl.when(has(*side))
            def _(side=side):
                halo_copy(which, side).start()

    def halo_wait(which):
        for side in SIDES:

            @pl.when(has(-side[0], -side[1]))
            def _(side=side):
                halo_copy(which, side).wait_recv()

    def assemble(which):
        for x in range(4):
            for pair in range(2):
                parts = [got[which, s, x, pair].astype(F32) for s in range(4)]
                for odd in range(2):
                    rows = [part[8 * odd : 8 * odd + 8] for part in parts]
                    field[which, 1 + x, 1 + 2 * pair + odd] = jnp.concatenate(rows, axis=0).astype(BF16)

    for k in range(1, 4):
        in_copy(VOL, k).wait_recv()
    assemble(VOL)
    halo_start(VOL)

    for k in range(1, 4):
        w_copy(k).wait_recv()
        pass_copy(k).start()
    for k in range(1, 4):
        pass_copy(k).wait_recv()

    def taps_of(which):
        parts = [w_got[s, which].astype(F32) for s in range(4)]
        groups = [
            jnp.concatenate([part[8 * a : 8 * a + 8] for part in parts], axis=0) for a in range(7)
        ]

        def tap(dx, dy, dz):
            t = (dx * 3 + dy) * 3 + dz
            return groups[t // 4][:, 32 * (t % 4) : 32 * (t % 4) + 32]

        return groups, tap

    def make_forward(which):
        groups, tap = taps_of(which)
        for dz in range(3):
            line = jnp.concatenate([tap(k // 3, k % 3, dz) for k in range(9)], axis=1)
            lhs[2 * which, 32 * dz : 32 * dz + 32] = line.astype(BF16)
        return groups

    def make_turned(which):
        _, tap = taps_of(which)
        zeros = jnp.zeros((32, 32), F32)
        for dx in range(3):
            lines = [
                jnp.concatenate([tap(2 - dx, 2 - dy, 2 - dz) for dz in range(3)] + [zeros], axis=1)
                for dy in range(3)
            ]
            lines.append(jnp.zeros((32, 128), F32))
            block = jnp.concatenate(lines, axis=0)
            lhs[2 * which + 1, :, 96 * dx : 96 * dx + 96] = block.T[:96, :96].astype(BF16)

    groups = make_forward(0)
    bias_all = groups[6][:, 96:97] + groups[6][:, 97:98] + groups[6][:, 98:99]
    make_turned(1)

    lane = iota((32, 128), 1)
    not_first = lane > 0
    not_last = lane < 127

    def shift_up(rows):
        return jnp.where(not_first, pltpu.roll(rows, 1, 1), 0.0)

    def shift_down(rows):
        return jnp.where(not_last, pltpu.roll(rows, 127, 1), 0.0)

    def window(which, x, dx):
        return jnp.concatenate(
            [field[which, x + dx, y : y + 3].reshape(96, 128) for y in range(4)], axis=1
        )

    def conv(which, number, x):
        block = jnp.concatenate([window(which, x, dx) for dx in range(3)], axis=0)
        sums = jnp.dot(lhs[number], block, preferred_element_type=F32)
        lines = []
        for y in range(4):
            part = sums[:, 128 * y : 128 * y + 128]
            lines.append(part[32:64] + shift_up(part[0:32]) + shift_down(part[64:96]))
        return lines

    for k in range(1, 4):
        in_copy(COT, k).wait_recv()
    assemble(COT)
    halo_start(COT)
    halo_wait(VOL)
    for x in range(4):
        for y, line in enumerate(conv(VOL, 0, x)):
            act = line + bias_all
            pre_act[x, y] = act
            field[HID, 1 + x, 1 + y] = (act / (1.0 + jnp.exp(-act))).astype(BF16)
    halo_start(HID)

    make_forward(1)
    make_turned(0)
    halo_wait(COT)
    bias_sum = jnp.zeros((32, 128), F32)
    for x in range(4):
        for y, line in enumerate(conv(COT, 3, x)):
            act = pre_act[x, y]
            sig = 1.0 / (1.0 + jnp.exp(-act))
            value = (line * sig * (1.0 + act * (1.0 - sig))).astype(BF16)
            bias_sum = bias_sum + value.astype(F32)
            field[PRE, 1 + x, 1 + y] = value
    halo_start(PRE)

    def shifted(which, x, flip):
        columns = []
        for y in range(4):
            rows = field[which, 1 + x, 1 + y].astype(F32)
            up, down = shift_up(rows), shift_down(rows)
            trio = [down, rows, up] if flip else [up, rows, down]
            columns.append(jnp.concatenate(trio, axis=0).astype(BF16))
        return jnp.concatenate(columns, axis=1)

    along = (((1,), (1,)), ((), ()))

    acc_one = [jnp.zeros((96, 96), F32) for _ in range(3)]
    acc_two = [jnp.zeros((96, 96), F32) for _ in range(3)]
    for x in range(4):
        own_pre = shifted(PRE, x, True)
        own_hid = shifted(HID, x, False)
        for dx in range(3):
            acc_one[dx] = acc_one[dx] + lax.dot_general(
                own_pre, window(VOL, x, dx), along, preferred_element_type=F32
            )
            acc_two[dx] = acc_two[dx] + lax.dot_general(
                window(COT, x, dx), own_hid, along, preferred_element_type=F32
            )
    bias_own = jnp.sum(bias_sum, axis=1, keepdims=True)
    for which, acc in enumerate((acc_one, acc_two)):
        for s in range(4):
            blocks = [acc[k // 3][32 * (k % 3) + 8 * s : 32 * (k % 3) + 8 * s + 8] for k in range(9)]
            tiles = []
            for k in range(6):
                cut = blocks[6 + k // 3][:, 32 * (k % 3) : 32 * (k % 3) + 32]
                tiles.append(jnp.concatenate([blocks[k], cut], axis=1))
            if which == 0:
                extra = jnp.broadcast_to(bias_own[8 * s : 8 * s + 8], (8, 32))
            else:
                extra = jnp.zeros((8, 32), F32)
            tiles.append(jnp.concatenate([blocks[8], extra], axis=1))
            tiles.append(jnp.zeros((8, 128), F32))
            for k in range(8):
                grad[which, 2 * k, s] = tiles[k][0:4]
                grad[which, 2 * k + 1, s] = tiles[k][4:8]

    core_copy = pltpu.make_async_remote_copy(
        src_ref=grad.at[1 - core],
        dst_ref=core_got,
        send_sem=core_send.at[0],
        recv_sem=core_recv.at[0],
        device_id={"gx": 2 * row + 1 - core},
        device_id_type=MESH,
    )
    core_copy.start()

    def out_copy(which, k):
        return pltpu.make_async_remote_copy(
            src_ref=out_stage.at[which, af_peer[k]],
            dst_ref=out_got.at[which, sub],
            send_sem=out_send.at[which, k],
            recv_sem=out_recv.at[which, k],
            device_id={"af": af_peer[k]},
            device_id_type=MESH,
        )

    def produce(which, source, number):
        for x in range(4):
            lines = conv(source, number, x)
            for pair in range(2):
                for s in range(4):
                    rows = [lines[2 * pair + odd][8 * s : 8 * s + 8] for odd in range(2)]
                    out_stage[which, s, x, pair] = jnp.concatenate(rows, axis=0).astype(BF16)
        out_got[which, pl.ds(sub, 1)] = out_stage[which, pl.ds(af, 1)]
        for k in (2, 1, 3):
            out_copy(which, k).start()

    halo_wait(HID)
    produce(0, HID, 2)

    pl.semaphore_wait(line_in, len(across))
    core_copy.wait_recv()
    core_sum[...] = grad[core] + core_got[...]
    plane_got[place] = core_sum[pl.ds(place * kept, kept)]

    def plane_copy(k):
        other_row, other_gy = at_place(k)
        return pltpu.make_async_remote_copy(
            src_ref=core_sum.at[pl.ds(((place + k) % plane) * kept, kept)],
            dst_ref=plane_got.at[place],
            send_sem=plane_send.at[k],
            recv_sem=plane_recv.at[k],
            device_id={"gx": 2 * other_row + core, "gy": other_gy},
            device_id_type=MESH,
        )

    for k in range(1, plane):
        plane_copy(k).start()

    halo_wait(PRE)
    produce(1, PRE, 1)

    for k in range(1, plane):
        plane_copy(k).wait_recv()
    line_stage[...] = sum([plane_got[i] for i in range(1, plane)], plane_got[0])

    at_line = high * 4 + af
    line_got[at_line] = line_stage[:, pl.ds(af, 1)].reshape(kept, 4, 128)

    def line_copy(k):
        other = af_peer[k % 4]
        return pltpu.make_async_remote_copy(
            src_ref=line_stage.at[:, other],
            dst_ref=line_got.at[at_line],
            send_sem=line_send.at[k],
            recv_sem=line_recv.at[k],
            device_id={"gy": ((high + k // 4) % 2) * n_x + col, "af": other},
            device_id_type=MESH,
        )

    for k in range(1, 8):
        line_copy(k).start()

    def finish(which, target):
        for k in range(1, 4):
            out_copy(which, k).wait_recv()
        block = jnp.concatenate(
            [
                jnp.concatenate([out_got[which, j, x].reshape(32, 128) for j in range(4)], axis=0)
                for x in range(4)
            ],
            axis=1,
        )
        moved = jnp.dot(from_wire, block, preferred_element_type=F32).astype(BF16)
        for x in range(4):
            target[:, x] = moved[:, 128 * x : 128 * x + 128].reshape(8, 16, 128)

    finish(0, out)
    stores[0].start()
    scale = 1.0 / math.sqrt(4 * n_gx * 16 * n_gy * 128)

    def last_copy(k, same):
        other_row, other_gy = at_place(k)
        part = final.at[core, pl.ds(place * kept, kept)]
        return pltpu.make_async_remote_copy(
            src_ref=part,
            dst_ref=part,
            send_sem=last_send.at[2 * k + same],
            recv_sem=last_recv.at[2 * k + same],
            device_id={"gx": 2 * other_row + (core if same else 1 - core), "gy": other_gy},
            device_id_type=MESH,
        )

    others = [(k, same) for k in range(plane) for same in (1, 0)][1:]
    for k in range(1, 8):
        line_copy(k).wait_recv()
    total = sum([line_got[i] for i in range(1, 8)], line_got[0])
    final[core, pl.ds(place * kept, kept)] = total * scale
    for k, same in others:
        last_copy(k, same).start()

    finish(1, in_grad)
    stores[1].start()

    for k, same in others:
        last_copy(k, same).wait_recv()

    for kind in range(2):
        tiles = [jnp.concatenate([final[kind, 2 * k], final[kind, 2 * k + 1]], axis=0) for k in range(7)]
        if kind == 0:
            bias_total = tiles[6][:, 96:97]
        for a in range(3):
            for b in range(3):
                for c in range(3):
                    k = 3 * a + b
                    if k < 6:
                        tap = tiles[k][:, 32 * c : 32 * c + 32]
                    elif k < 8:
                        tap = tiles[3 * (k - 6) + c][:, 96:128]
                    else:
                        tap = tiles[6][:, 32 * c : 32 * c + 32]
                    if kind == 0:
                        g_one[a, c, b] = tap
                    else:
                        g_two[2 - a, 2 - b, c] = tap
    g_bias[...] = jnp.sum(jnp.where(diag, bias_total, 0.0), axis=0, keepdims=True)
    for copy in stores[2:]:
        copy.start()

    for k in range(1, 4):
        in_copy(COT, k).wait_send()
        w_copy(k).wait_send()
        out_copy(0, k).wait_send()
        out_copy(1, k).wait_send()
        pass_copy(k).wait_send()
    for which in (VOL, COT, HID, PRE):
        for side in SIDES:

            @pl.when(has(*side))
            def _(which=which, side=side):
                halo_copy(which, side).wait_send()

    core_copy.wait_send()
    for k in range(1, plane):
        plane_copy(k).wait_send()
    for k in range(1, 8):
        line_copy(k).wait_send()
    for k, same in others:
        last_copy(k, same).wait_send()
    for copy in stores:
        copy.wait()


def store(*refs):
    sources, targets, held, sems = refs[:5], refs[5:10], refs[10:15], refs[15]
    loads = [pltpu.make_async_copy(sources[i], held[i], sems.at[0, i]) for i in range(5)]
    copies = [pltpu.make_async_copy(held[i], targets[i], sems.at[1, i]) for i in range(5)]
    for load in loads:
        load.start()
    for load, copy in zip(loads, copies):
        load.wait()
        copy.start()
    for copy in copies:
        copy.wait()


def body(dims, volume, weight_one, bias_one, weight_two, cotangent):
    plane = (dims[0] // 2) * (dims[1] // 2)
    as_taps = (2, 3, 4, 0, 1)
    dma = pltpu.SemaphoreType.DMA
    out, in_grad, g_one, g_bias, g_two = pl.pallas_call(
        functools.partial(kernel, dims),
        out_shape=(
            jax.ShapeDtypeStruct((8, 4, 16, 128), BF16),
            jax.ShapeDtypeStruct((8, 4, 16, 128), BF16),
            jax.ShapeDtypeStruct((3, 3, 3, 8, 32), F32),
            jax.ShapeDtypeStruct((1, 8), F32),
            jax.ShapeDtypeStruct((3, 3, 3, 8, 32), F32),
        ),
        in_specs=[pl.BlockSpec(memory_space=pltpu.HBM)] * 5,
        out_specs=[pl.BlockSpec(memory_space=pltpu.HBM)] * 5,
        scratch_shapes=[
            pltpu.VMEM((8, 4, 16, 128), BF16),
            pltpu.VMEM((8, 4, 16, 128), BF16),
            pltpu.VMEM((3, 3, 3, 8, 32), F32),
            pltpu.VMEM((1, 8), F32),
            pltpu.VMEM((3, 3, 3, 8, 32), F32),
            pltpu.VMEM((8, 4, 16, 128), BF16),
            pltpu.VMEM((3, 3, 3, 8, 32), BF16),
            pltpu.VMEM((1, 8), F32),
            pltpu.VMEM((3, 3, 3, 8, 32), BF16),
            pltpu.VMEM((8, 4, 16, 128), BF16),
            pltpu.VMEM((2, 4, 4, 2, 16, 128), BF16),
            pltpu.VMEM((2, 4, 4, 2, 16, 128), BF16),
            pltpu.VMEM((2, 64, 128), BF16),
            pltpu.VMEM((4, 2, 64, 128), BF16),
            pltpu.VMEM((4, 6, 6, 32, 128), BF16),
            pltpu.VMEM((4, 4, 32, 128), F32),
            pltpu.VMEM((4, 96, 288), BF16),
            pltpu.VMEM((2, 4, 4, 2, 16, 128), BF16),
            pltpu.VMEM((2, 4, 4, 2, 16, 128), BF16),
            pltpu.VMEM((2, 16, 4, 4, 128), F32),
            pltpu.VMEM((16, 4, 4, 128), F32),
            pltpu.VMEM((16, 4, 4, 128), F32),
            pltpu.VMEM((plane, 16 // plane, 4, 4, 128), F32),
            pltpu.VMEM((16 // plane, 4, 4, 128), F32),
            pltpu.VMEM((8, 16 // plane, 4, 128), F32),
            pltpu.VMEM((2, 16, 4, 128), F32),
            dma((2, 4)), dma((2, 4)), dma((4,)), dma((4,)), dma((4,)), dma((4,)),
            dma((4, 8)), dma((4, 8)), dma((2, 4)), dma((2, 4)),
            dma((1,)), dma((1,)), dma((plane,)), dma((plane,)), dma((8,)), dma((8,)), dma((2 * plane,)), dma((2 * plane,)),
            dma((5,)), dma((5,)), pltpu.SemaphoreType.REGULAR,
        ],
        compiler_params=pltpu.CompilerParams(
            collective_id=0, has_side_effects=True, vmem_limit_bytes=60 * 1024 * 1024
        ),
    )(
        volume,
        jnp.transpose(weight_one, as_taps),
        bias_one.reshape(1, 8),
        jnp.transpose(weight_two, as_taps),
        cotangent,
    )
    results = (out, in_grad, g_one, g_bias, g_two)
    out, in_grad, g_one, g_bias, g_two = pl.pallas_call(
        store,
        out_shape=tuple(jax.ShapeDtypeStruct(part.shape, part.dtype) for part in results),
        in_specs=[pl.BlockSpec(memory_space=pltpu.HBM)] * 5,
        out_specs=[pl.BlockSpec(memory_space=pltpu.HBM)] * 5,
        scratch_shapes=[pltpu.VMEM(part.shape, part.dtype) for part in results] + [dma((2, 5))],
        compiler_params=pltpu.CompilerParams(vmem_limit_bytes=60 * 1024 * 1024),
    )(*results)
    as_given = (3, 4, 0, 1, 2)
    return (
        out,
        in_grad,
        jnp.transpose(g_one, as_given),
        g_bias.reshape(8),
        jnp.transpose(g_two, as_given),
    )


def solution(mesh):
    dims = (mesh.shape["gx"], mesh.shape["gy"])
    return jax.shard_map(
        functools.partial(body, dims),
        mesh=mesh,
        in_specs=(
            P("af", "gx", "gy", None),
            P("af", None, None, None, None),
            P("af"),
            P("af", None, None, None, None),
            P("af", "gx", "gy", None),
        ),
        out_specs=(
            P("af", "gx", "gy", None),
            P("af", "gx", "gy", None),
            P("af", None, None, None, None),
            P("af"),
            P("af", None, None, None, None),
        ),
        check_vma=False,
    )
```

```python
import functools
import math

import jax
import jax.numpy as jnp
from jax import lax
from jax.experimental import pallas as pl
from jax.experimental.pallas import tpu as pltpu
from jax.sharding import PartitionSpec as P

MESH = pl.DeviceIdType.MESH
F32 = jnp.float32
BF16 = jnp.bfloat16

VOL, COT, HID, PRE = 0, 1, 2, 3
SIDES = [(-1, -1), (-1, 1), (1, -1), (1, 1), (0, -1), (0, 1), (-1, 0), (1, 0)]
FAR = (10, 9, 11, 6, 14, 8, 2, 5, 7, 13, 15, 1, 3, 4, 12)
SEND = {-1: (1, 1), 0: (1, 4), 1: (4, 1)}
EDGE = {-1: (0, 1), 0: (1, 4), 1: (5, 1)}
LAND = {-1: (5, 1), 0: (1, 4), 1: (0, 1)}


def iota(shape, dim):
    return lax.broadcasted_iota(jnp.int32, shape, dim)


def kernel(
    dims,
    vol_in, w_one_in, bias_in, w_two_in, cot_in,
    out_to, in_grad_to, final_to,
    out, in_grad,
    vol, w_one, bias, w_two, cot,
    stage, got, w_stage, w_got, field, pre_act, lhs,
    out_stage, out_got, grad, core_got, core_sum, plane_got, line_stage, line_got, final,
    in_send, in_recv, w_send, w_recv, pass_send, pass_recv, halo_send, halo_recv, out_send, out_recv,
    core_send, core_recv, plane_send, plane_recv, line_send, line_recv, last_send, last_recv, load_sem, store_sem, line_in,
):
    loads = [
        pltpu.make_async_copy(source, target, load_sem.at[i])
        for i, (source, target) in enumerate(
            ((vol_in, vol), (w_one_in, w_one), (w_two_in, w_two), (bias_in, bias), (cot_in, cot))
        )
    ]
    for load in loads:
        load.start()
    stores = [
        pltpu.make_async_copy(source, target, store_sem.at[i])
        for i, (source, target) in enumerate(
            ((out, out_to), (in_grad, in_grad_to), (final, final_to))
        )
    ]
    n_gx, n_gy = dims
    n_y, n_x = n_gx // 2, n_gy // 2
    gx, gy, af = lax.axis_index("gx"), lax.axis_index("gy"), lax.axis_index("af")
    row, core = gx // 2, gx % 2
    col, high = gy % n_x, gy // n_x

    def turned(at):
        even = (at % 2) == 0
        upper = at >= n_x
        return jnp.logical_xor(even, upper)

    def sub_of(at_af, at_gy):
        return jnp.where(turned(at_gy), 3 - at_af, at_af)

    sub = sub_of(af, gy)

    def y_neighbour(step):
        if step == 0:
            return gy, af
        inside = (sub < 3) if step > 0 else (sub > 0)
        gy_new = jnp.where(inside, gy, (gy + step + n_gy) % n_gy)
        sub_new = jnp.where(inside, sub + step, 0 if step > 0 else 3)
        return gy_new, sub_of(sub_new, gy_new)

    def has(dx, dy):
        checks = []
        if dx < 0:
            checks.append(gx > 0)
        if dx > 0:
            checks.append(gx < n_gx - 1)
        if dy < 0:
            checks.append(jnp.logical_or(gy > 0, sub > 0))
        if dy > 0:
            checks.append(jnp.logical_or(gy < n_gy - 1, sub < 3))
        if len(checks) == 1:
            return checks[0]
        return jnp.logical_and(checks[0], checks[1])

    ring = {step: y_neighbour(step) for step in (-1, 0, 1)}
    neighbour = {(dx, dy): {"gx": gx + dx, "gy": ring[dy][0], "af": ring[dy][1]} for dx, dy in SIDES}
    af_peer = [(af + k) % 4 for k in range(4)]

    plane = n_y * n_x
    place = row * n_x + col
    kept = 16 // plane
    far = [k for k in FAR if k < plane]

    def at_place(k):
        other = (place + k) % plane
        return other // n_x, high * n_x + other % n_x

    for side in SIDES:
        (fx, cx), (fy, cy) = EDGE[side[0]], EDGE[side[1]]
        field[:, fx : fx + cx, fy : fy + cy] = jnp.zeros((4, cx, cy, 32, 128), BF16)

    barrier = pltpu.get_barrier_semaphore()
    across = [{"gy": high * n_x + (col + k) % n_x} for k in range(1, n_x)]
    across += [{"gy": (1 - high) * n_x + col}]
    partners = across + [{"af": af_peer[k]} for k in range(1, 4)]
    partners += [{"gx": 2 * ((row + k) % n_y) + core} for k in range(1, n_y)]
    for dx, dy in SIDES:
        partners.append({"gx": (gx + dx + n_gx) % n_gx, "gy": ring[dy][0], "af": ring[dy][1]})
    for partner in partners:
        pl.semaphore_signal(barrier, inc=1, device_id=partner, device_id_type=MESH)

    r, q = iota((128, 128), 0), iota((128, 128), 1)
    to_wire = jnp.where(q == (r % 8) * 16 + r // 8, 1.0, 0.0).astype(BF16)
    from_wire = jnp.where(q == (r % 16) * 8 + r // 16, 1.0, 0.0).astype(BF16)

    def stage_input(which, source):
        block = jnp.concatenate([source[:, x].reshape(128, 128) for x in range(4)], axis=1)
        moved = jnp.dot(to_wire, block, preferred_element_type=F32).astype(BF16)
        for x in range(4):
            for j in range(4):
                part = moved[32 * j : 32 * j + 32, 128 * x : 128 * x + 128]
                stage[which, j, x] = part.reshape(2, 16, 128)
        got[which, pl.ds(af, 1)] = stage[which, pl.ds(sub, 1)]

    def in_copy(which, k):
        return pltpu.make_async_remote_copy(
            src_ref=stage.at[which, sub_of(af_peer[k], gy)],
            dst_ref=got.at[which, af],
            send_sem=in_send.at[which, k],
            recv_sem=in_recv.at[which, k],
            device_id={"af": af_peer[k]},
            device_id_type=MESH,
        )

    def w_copy(k):
        return pltpu.make_async_remote_copy(
            src_ref=w_stage.at[core],
            dst_ref=w_got.at[af, core],
            send_sem=w_send.at[k],
            recv_sem=w_recv.at[k],
            device_id={"af": af_peer[k]},
            device_id_type=MESH,
        )

    def pass_copy(k):
        origin = (af + 4 - k) % 4
        return pltpu.make_async_remote_copy(
            src_ref=w_got.at[origin, core],
            dst_ref=w_got.at[origin, core],
            send_sem=pass_send.at[k],
            recv_sem=pass_recv.at[k],
            device_id={"gx": 2 * row + 1 - core},
            device_id_type=MESH,
        )

    loads[0].wait()
    stage_input(VOL, vol)
    for load in loads[1:]:
        load.wait()
    diag = iota((8, 8), 0) == iota((8, 8), 1)
    bias_col = jnp.sum(jnp.where(diag, bias[...], 0.0), axis=1, keepdims=True)
    part_a = bias_col.astype(BF16).astype(F32)
    part_b = (bias_col - part_a).astype(BF16).astype(F32)
    part_c = (bias_col - part_a) - part_b
    lane32 = iota((8, 32), 1)
    spare = jnp.where(lane32 == 0, part_a, jnp.where(lane32 == 1, part_b, jnp.where(lane32 == 2, part_c, 0.0)))
    for which, weight in enumerate((w_one, w_two)):
        groups = []
        for a in range(7):
            taps = []
            for b in range(4):
                t = 4 * a + b
                taps.append(weight[t // 9, (t // 3) % 3, t % 3].astype(F32) if t < 27 else spare)
            groups.append(jnp.concatenate(taps, axis=1))
        groups.append(jnp.zeros((8, 128), F32))
        packed = jnp.concatenate(groups, axis=0).astype(BF16)
        w_stage[which] = packed
        w_got[af, which] = packed
    pl.semaphore_wait(barrier, len(partners))
    for k in (2, 1, 3):
        in_copy(VOL, k).start()
    for partner in across:
        pl.semaphore_signal(line_in, inc=1, device_id=partner, device_id_type=MESH)

    for k in (2, 1, 3):
        w_copy(k).start()
    stage_input(COT, cot)
    for k in (2, 1, 3):
        in_copy(VOL, k).wait_send()
    for k in (2, 1, 3):
        in_copy(COT, k).start()

    def halo_copy(which, side):
        number = SIDES.index(side)
        (sx, nx), (sy, ny) = SEND[side[0]], SEND[side[1]]
        (lx, _), (ly, _) = LAND[side[0]], LAND[side[1]]
        return pltpu.make_async_remote_copy(
            src_ref=field.at[which, sx : sx + nx, sy : sy + ny],
            dst_ref=field.at[which, lx : lx + nx, ly : ly + ny],
            send_sem=halo_send.at[which, number],
            recv_sem=halo_recv.at[which, number],
            device_id=neighbour[side],
            device_id_type=MESH,
        )

    def halo_start(which):
        for side in SIDES:

            @pl.when(has(*side))
            def _(side=side):
                halo_copy(which, side).start()

    def halo_wait(which):
        for side in SIDES:

            @pl.when(has(-side[0], -side[1]))
            def _(side=side):
                halo_copy(which, side).wait_recv()

    def assemble(which):
        for x in range(4):
            for pair in range(2):
                parts = [got[which, s, x, pair].astype(F32) for s in range(4)]
                for odd in range(2):
                    rows = [part[8 * odd : 8 * odd + 8] for part in parts]
                    field[which, 1 + x, 1 + 2 * pair + odd] = jnp.concatenate(rows, axis=0).astype(BF16)

    for k in range(1, 4):
        in_copy(VOL, k).wait_recv()
    assemble(VOL)
    halo_start(VOL)

    for k in range(1, 4):
        w_copy(k).wait_recv()
        pass_copy(k).start()
    for k in range(1, 4):
        in_copy(COT, k).wait_recv()
    assemble(COT)
    halo_start(COT)
    for k in range(1, 4):
        pass_copy(k).wait_recv()

    def taps_of(which):
        parts = [w_got[s, which].astype(F32) for s in range(4)]
        groups = [
            jnp.concatenate([part[8 * a : 8 * a + 8] for part in parts], axis=0) for a in range(7)
        ]

        def tap(dx, dy, dz):
            t = (dx * 3 + dy) * 3 + dz
            return groups[t // 4][:, 32 * (t % 4) : 32 * (t % 4) + 32]

        return groups, tap

    def make_forward(which):
        groups, tap = taps_of(which)
        for dz in range(3):
            line = jnp.concatenate([tap(k // 3, k % 3, dz) for k in range(9)], axis=1)
            lhs[2 * which, 32 * dz : 32 * dz + 32] = line.astype(BF16)
        return groups

    def make_turned(which):
        _, tap = taps_of(which)
        zeros = jnp.zeros((32, 32), F32)
        for dx in range(3):
            lines = [
                jnp.concatenate([tap(2 - dx, 2 - dy, 2 - dz) for dz in range(3)] + [zeros], axis=1)
                for dy in range(3)
            ]
            lines.append(jnp.zeros((32, 128), F32))
            block = jnp.concatenate(lines, axis=0)
            lhs[2 * which + 1, :, 96 * dx : 96 * dx + 96] = block.T[:96, :96].astype(BF16)

    groups = make_forward(0)
    bias_all = groups[6][:, 96:97] + groups[6][:, 97:98] + groups[6][:, 98:99]
    make_turned(1)

    lane = iota((32, 128), 1)
    not_first = lane > 0
    not_last = lane < 127

    def shift_up(rows):
        return jnp.where(not_first, pltpu.roll(rows, 1, 1), 0.0)

    def shift_down(rows):
        return jnp.where(not_last, pltpu.roll(rows, 127, 1), 0.0)

    def window(which, x, dx):
        return jnp.concatenate(
            [field[which, x + dx, y : y + 3].reshape(96, 128) for y in range(4)], axis=1
        )

    def conv(which, number, x):
        block = jnp.concatenate([window(which, x, dx) for dx in range(3)], axis=0)
        sums = jnp.dot(lhs[number], block, preferred_element_type=F32)
        lines = []
        for y in range(4):
            part = sums[:, 128 * y : 128 * y + 128]
            lines.append(part[32:64] + shift_up(part[0:32]) + shift_down(part[64:96]))
        return lines

    halo_wait(VOL)
    for x in range(4):
        for y, line in enumerate(conv(VOL, 0, x)):
            act = line + bias_all
            pre_act[x, y] = act
            field[HID, 1 + x, 1 + y] = (act / (1.0 + jnp.exp(-act))).astype(BF16)
    halo_start(HID)

    make_forward(1)
    make_turned(0)
    halo_wait(COT)
    bias_sum = jnp.zeros((32, 128), F32)
    for x in range(4):
        for y, line in enumerate(conv(COT, 3, x)):
            act = pre_act[x, y]
            sig = 1.0 / (1.0 + jnp.exp(-act))
            value = (line * sig * (1.0 + act * (1.0 - sig))).astype(BF16)
            bias_sum = bias_sum + value.astype(F32)
            field[PRE, 1 + x, 1 + y] = value
    halo_start(PRE)

    def shifted(which, x, flip):
        columns = []
        for y in range(4):
            rows = field[which, 1 + x, 1 + y].astype(F32)
            up, down = shift_up(rows), shift_down(rows)
            trio = [down, rows, up] if flip else [up, rows, down]
            columns.append(jnp.concatenate(trio, axis=0).astype(BF16))
        return jnp.concatenate(columns, axis=1)

    along = (((1,), (1,)), ((), ()))

    acc_one = [jnp.zeros((96, 96), F32) for _ in range(3)]
    acc_two = [jnp.zeros((96, 96), F32) for _ in range(3)]
    for x in range(4):
        own_pre = shifted(PRE, x, True)
        own_hid = shifted(HID, x, False)
        for dx in range(3):
            acc_one[dx] = acc_one[dx] + lax.dot_general(
                own_pre, window(VOL, x, dx), along, preferred_element_type=F32
            )
            acc_two[dx] = acc_two[dx] + lax.dot_general(
                window(COT, x, dx), own_hid, along, preferred_element_type=F32
            )
    bias_own = jnp.sum(bias_sum, axis=1, keepdims=True)
    for which, acc in enumerate((acc_one, acc_two)):
        for s in range(4):
            blocks = [acc[k // 3][32 * (k % 3) + 8 * s : 32 * (k % 3) + 8 * s + 8] for k in range(9)]
            tiles = []
            for k in range(6):
                cut = blocks[6 + k // 3][:, 32 * (k % 3) : 32 * (k % 3) + 32]
                tiles.append(jnp.concatenate([blocks[k], cut], axis=1))
            if which == 0:
                extra = jnp.broadcast_to(bias_own[8 * s : 8 * s + 8], (8, 32))
            else:
                extra = jnp.zeros((8, 32), F32)
            tiles.append(jnp.concatenate([blocks[8], extra], axis=1))
            tiles.append(jnp.zeros((8, 128), F32))
            for k in range(8):
                grad[which, 2 * k, s] = tiles[k][0:4]
                grad[which, 2 * k + 1, s] = tiles[k][4:8]

    core_copy = pltpu.make_async_remote_copy(
        src_ref=grad.at[1 - core],
        dst_ref=core_got,
        send_sem=core_send.at[0],
        recv_sem=core_recv.at[0],
        device_id={"gx": 2 * row + 1 - core},
        device_id_type=MESH,
    )
    core_copy.start()

    def out_copy(which, k):
        return pltpu.make_async_remote_copy(
            src_ref=out_stage.at[which, af_peer[k]],
            dst_ref=out_got.at[which, sub],
            send_sem=out_send.at[which, k],
            recv_sem=out_recv.at[which, k],
            device_id={"af": af_peer[k]},
            device_id_type=MESH,
        )

    def produce(which, source, number):
        for x in range(4):
            lines = conv(source, number, x)
            for pair in range(2):
                for s in range(4):
                    rows = [lines[2 * pair + odd][8 * s : 8 * s + 8] for odd in range(2)]
                    out_stage[which, s, x, pair] = jnp.concatenate(rows, axis=0).astype(BF16)
        out_got[which, pl.ds(sub, 1)] = out_stage[which, pl.ds(af, 1)]
        for k in (2, 1, 3):
            out_copy(which, k).start()

    halo_wait(HID)
    produce(0, HID, 2)

    pl.semaphore_wait(line_in, len(across))
    core_copy.wait_recv()
    core_sum[...] = grad[core] + core_got[...]
    plane_got[place] = core_sum[pl.ds(place * kept, kept)]

    def plane_copy(k):
        other_row, other_gy = at_place(k)
        return pltpu.make_async_remote_copy(
            src_ref=core_sum.at[pl.ds(((place + k) % plane) * kept, kept)],
            dst_ref=plane_got.at[place],
            send_sem=plane_send.at[k],
            recv_sem=plane_recv.at[k],
            device_id={"gx": 2 * other_row + core, "gy": other_gy},
            device_id_type=MESH,
        )

    for k in far:
        plane_copy(k).start()

    halo_wait(PRE)
    produce(1, PRE, 1)

    for k in range(1, plane):
        plane_copy(k).wait_recv()
    line_stage[...] = sum([plane_got[i] for i in range(1, plane)], plane_got[0])

    at_line = high * 4 + af
    line_got[core, at_line] = line_stage[:, pl.ds(af, 1)].reshape(kept, 4, 128)

    def line_copy(k, same):
        other = af_peer[k % 4]
        return pltpu.make_async_remote_copy(
            src_ref=line_stage.at[:, other],
            dst_ref=line_got.at[core, at_line],
            send_sem=line_send.at[2 * k + same],
            recv_sem=line_recv.at[2 * k + same],
            device_id={
                "gx": 2 * row + (core if same else 1 - core),
                "gy": ((high + k // 4) % 2) * n_x + col,
                "af": other,
            },
            device_id_type=MESH,
        )

    line_others = [(k, same) for k in (4, 5, 6, 7, 2, 3, 1) for same in (1, 0)] + [(0, 0)]
    for k, same in line_others:
        line_copy(k, same).start()

    def finish(which, target):
        for k in range(1, 4):
            out_copy(which, k).wait_recv()
        block = jnp.concatenate(
            [
                jnp.concatenate([out_got[which, j, x].reshape(32, 128) for j in range(4)], axis=0)
                for x in range(4)
            ],
            axis=1,
        )
        moved = jnp.dot(from_wire, block, preferred_element_type=F32).astype(BF16)
        for x in range(4):
            target[:, x] = moved[:, 128 * x : 128 * x + 128].reshape(8, 16, 128)

    finish(0, out)
    stores[0].start()
    scale = 1.0 / math.sqrt(4 * n_gx * 16 * n_gy * 128)

    def last_copy(k):
        other_row, other_gy = at_place(k)
        part = final.at[place]
        return pltpu.make_async_remote_copy(
            src_ref=part,
            dst_ref=part,
            send_sem=last_send.at[k],
            recv_sem=last_recv.at[k],
            device_id={"gx": 2 * other_row + core, "gy": other_gy},
            device_id_type=MESH,
        )

    for k, same in line_others:
        line_copy(k, same).wait_recv()
    for kind in range(2):
        total = sum([line_got[kind, i] for i in range(1, 8)], line_got[kind, 0])
        final[place, pl.ds(kind * kept, kept)] = total * scale
    for k in far:
        last_copy(k).start()

    finish(1, in_grad)
    stores[1].start()

    for k in range(1, plane):
        last_copy(k).wait_recv()

    stores[2].start()

    for k in range(1, 4):
        in_copy(COT, k).wait_send()
        w_copy(k).wait_send()
        out_copy(0, k).wait_send()
        out_copy(1, k).wait_send()
        pass_copy(k).wait_send()
    for which in (VOL, COT, HID, PRE):
        for side in SIDES:

            @pl.when(has(*side))
            def _(which=which, side=side):
                halo_copy(which, side).wait_send()

    core_copy.wait_send()
    for k in range(1, plane):
        plane_copy(k).wait_send()
    for k, same in line_others:
        line_copy(k, same).wait_send()
    for k in range(1, plane):
        last_copy(k).wait_send()
    for copy in stores:
        copy.wait()


def store(
    kept, out_in, in_grad_in, final_in, out_to, in_grad_to, g_one_to, g_bias_to, g_two_to,
    out, in_grad, final, g_one, g_bias, g_two, sems,
):
    loads = [
        pltpu.make_async_copy(source, target, sems.at[0, i])
        for i, (source, target) in enumerate(((final_in, final), (out_in, out), (in_grad_in, in_grad)))
    ]
    stores = [
        pltpu.make_async_copy(source, target, sems.at[1, i])
        for i, (source, target) in enumerate(
            ((out, out_to), (in_grad, in_grad_to), (g_one, g_one_to), (g_bias, g_bias_to), (g_two, g_two_to))
        )
    ]
    for load in loads:
        load.start()
    loads[0].wait()
    diag = iota((8, 8), 0) == iota((8, 8), 1)
    for kind in range(2):
        halves = [final[k // kept, kind * kept + k % kept] for k in range(14)]
        tiles = [jnp.concatenate(halves[2 * k : 2 * k + 2], axis=0) for k in range(7)]
        if kind == 0:
            bias_total = tiles[6][:, 96:97]
        for a in range(3):
            for b in range(3):
                for c in range(3):
                    k = 3 * a + b
                    if k < 6:
                        tap = tiles[k][:, 32 * c : 32 * c + 32]
                    elif k < 8:
                        tap = tiles[3 * (k - 6) + c][:, 96:128]
                    else:
                        tap = tiles[6][:, 32 * c : 32 * c + 32]
                    if kind == 0:
                        g_one[a, c, b] = tap
                    else:
                        g_two[2 - a, 2 - b, c] = tap
    g_bias[...] = jnp.sum(jnp.where(diag, bias_total, 0.0), axis=0, keepdims=True)
    for copy in stores[2:]:
        copy.start()
    for load, copy in zip(loads[1:], stores):
        load.wait()
        copy.start()
    for copy in stores:
        copy.wait()


def body(dims, volume, weight_one, bias_one, weight_two, cotangent):
    plane = (dims[0] // 2) * (dims[1] // 2)
    as_taps = (2, 3, 4, 0, 1)
    dma = pltpu.SemaphoreType.DMA
    cells = jax.ShapeDtypeStruct((8, 4, 16, 128), BF16)
    taps = jax.ShapeDtypeStruct((3, 3, 3, 8, 32), F32)
    dense = jax.ShapeDtypeStruct((plane, 2 * (16 // plane), 4, 128), F32)
    results = pl.pallas_call(
        functools.partial(kernel, dims),
        out_shape=(cells, cells, dense),
        in_specs=[pl.BlockSpec(memory_space=pltpu.HBM)] * 5,
        out_specs=[pl.BlockSpec(memory_space=pltpu.HBM)] * 3,
        scratch_shapes=[
            pltpu.VMEM((8, 4, 16, 128), BF16),
            pltpu.VMEM((8, 4, 16, 128), BF16),
            pltpu.VMEM((8, 4, 16, 128), BF16),
            pltpu.VMEM((3, 3, 3, 8, 32), BF16),
            pltpu.VMEM((1, 8), F32),
            pltpu.VMEM((3, 3, 3, 8, 32), BF16),
            pltpu.VMEM((8, 4, 16, 128), BF16),
            pltpu.VMEM((2, 4, 4, 2, 16, 128), BF16),
            pltpu.VMEM((2, 4, 4, 2, 16, 128), BF16),
            pltpu.VMEM((2, 64, 128), BF16),
            pltpu.VMEM((4, 2, 64, 128), BF16),
            pltpu.VMEM((4, 6, 6, 32, 128), BF16),
            pltpu.VMEM((4, 4, 32, 128), F32),
            pltpu.VMEM((4, 96, 288), BF16),
            pltpu.VMEM((2, 4, 4, 2, 16, 128), BF16),
            pltpu.VMEM((2, 4, 4, 2, 16, 128), BF16),
            pltpu.VMEM((2, 16, 4, 4, 128), F32),
            pltpu.VMEM((16, 4, 4, 128), F32),
            pltpu.VMEM((16, 4, 4, 128), F32),
            pltpu.VMEM((plane, 16 // plane, 4, 4, 128), F32),
            pltpu.VMEM((16 // plane, 4, 4, 128), F32),
            pltpu.VMEM((2, 8, 16 // plane, 4, 128), F32),
            pltpu.VMEM((plane, 2 * (16 // plane), 4, 128), F32),
            dma((2, 4)), dma((2, 4)), dma((4,)), dma((4,)), dma((4,)), dma((4,)),
            dma((4, 8)), dma((4, 8)), dma((2, 4)), dma((2, 4)),
            dma((1,)), dma((1,)), dma((plane,)), dma((plane,)), dma((16,)), dma((16,)), dma((plane,)), dma((plane,)),
            dma((5,)), dma((3,)), pltpu.SemaphoreType.REGULAR,
        ],
        compiler_params=pltpu.CompilerParams(
            collective_id=0, has_side_effects=True, vmem_limit_bytes=60 * 1024 * 1024
        ),
    )(
        volume,
        jnp.transpose(weight_one, as_taps),
        bias_one.reshape(1, 8),
        jnp.transpose(weight_two, as_taps),
        cotangent,
    )
    given = (cells, cells, taps, jax.ShapeDtypeStruct((1, 8), F32), taps)
    out, in_grad, g_one, g_bias, g_two = pl.pallas_call(
        functools.partial(store, 16 // plane),
        out_shape=given,
        in_specs=[pl.BlockSpec(memory_space=pltpu.HBM)] * 3,
        out_specs=[pl.BlockSpec(memory_space=pltpu.HBM)] * 5,
        scratch_shapes=[pltpu.VMEM(part.shape, part.dtype) for part in (cells, cells, dense, *given[2:])]
        + [dma((2, 5))],
        compiler_params=pltpu.CompilerParams(vmem_limit_bytes=60 * 1024 * 1024),
    )(*results)
    as_given = (3, 4, 0, 1, 2)
    return (
        out,
        in_grad,
        jnp.transpose(g_one, as_given),
        g_bias.reshape(8),
        jnp.transpose(g_two, as_given),
    )


def solution(mesh):
    dims = (mesh.shape["gx"], mesh.shape["gy"])
    return jax.shard_map(
        functools.partial(body, dims),
        mesh=mesh,
        in_specs=(
            P("af", "gx", "gy", None),
            P("af", None, None, None, None),
            P("af"),
            P("af", None, None, None, None),
            P("af", "gx", "gy", None),
        ),
        out_specs=(
            P("af", "gx", "gy", None),
            P("af", "gx", "gy", None),
            P("af", None, None, None, None),
            P("af"),
            P("af", None, None, None, None),
        ),
        check_vma=False,
    )
```

```python
import functools
import math

import jax
import jax.numpy as jnp
from jax import lax
from jax.experimental import pallas as pl
from jax.experimental.pallas import tpu as pltpu
from jax.sharding import PartitionSpec as P

MESH = pl.DeviceIdType.MESH
F32 = jnp.float32
BF16 = jnp.bfloat16

VOL, COT, HID, PRE = 0, 1, 2, 3
SIDES = [(-1, -1), (-1, 1), (1, -1), (1, 1), (0, -1), (0, 1), (-1, 0), (1, 0)]
FAR = (10, 9, 11, 6, 14, 8, 2, 5, 7, 13, 15, 1, 3, 4, 12)
SEND = {-1: (1, 1), 0: (1, 4), 1: (4, 1)}
EDGE = {-1: (0, 1), 0: (1, 4), 1: (5, 1)}
LAND = {-1: (5, 1), 0: (1, 4), 1: (0, 1)}


def iota(shape, dim):
    return lax.broadcasted_iota(jnp.int32, shape, dim)


def kernel(
    dims,
    vol_in, w_one_in, bias_in, w_two_in, cot_in,
    out_to, in_grad_to, final_to,
    out, in_grad,
    vol, w_one, bias, w_two, cot,
    stage, got, w_stage, w_got, field, pre_act, lhs,
    out_stage, out_got, grad, core_got, core_sum, plane_got, line_stage, line_got, final,
    in_send, in_recv, w_send, w_recv, pass_send, pass_recv, halo_send, halo_recv, out_send, out_recv,
    core_send, core_recv, plane_send, plane_recv, line_send, line_recv, last_send, last_recv, load_sem, store_sem, line_in,
):
    loads = [
        pltpu.make_async_copy(source, target, load_sem.at[i])
        for i, (source, target) in enumerate(
            ((vol_in, vol), (w_one_in, w_one), (w_two_in, w_two), (bias_in, bias), (cot_in, cot))
        )
    ]
    for load in loads:
        load.start()
    stores = [
        pltpu.make_async_copy(source, target, store_sem.at[i])
        for i, (source, target) in enumerate(
            ((out, out_to), (in_grad, in_grad_to), (final, final_to))
        )
    ]
    n_gx, n_gy = dims
    n_y, n_x = n_gx // 2, n_gy // 2
    gx, gy, af = lax.axis_index("gx"), lax.axis_index("gy"), lax.axis_index("af")
    row, core = gx // 2, gx % 2
    col, high = gy % n_x, gy // n_x

    def turned(at):
        even = (at % 2) == 0
        upper = at >= n_x
        return jnp.logical_xor(even, upper)

    def sub_of(at_af, at_gy):
        return jnp.where(turned(at_gy), 3 - at_af, at_af)

    sub = sub_of(af, gy)

    def y_neighbour(step):
        if step == 0:
            return gy, af
        inside = (sub < 3) if step > 0 else (sub > 0)
        gy_new = jnp.where(inside, gy, (gy + step + n_gy) % n_gy)
        sub_new = jnp.where(inside, sub + step, 0 if step > 0 else 3)
        return gy_new, sub_of(sub_new, gy_new)

    def has(dx, dy):
        checks = []
        if dx < 0:
            checks.append(gx > 0)
        if dx > 0:
            checks.append(gx < n_gx - 1)
        if dy < 0:
            checks.append(jnp.logical_or(gy > 0, sub > 0))
        if dy > 0:
            checks.append(jnp.logical_or(gy < n_gy - 1, sub < 3))
        if len(checks) == 1:
            return checks[0]
        return jnp.logical_and(checks[0], checks[1])

    ring = {step: y_neighbour(step) for step in (-1, 0, 1)}
    neighbour = {(dx, dy): {"gx": gx + dx, "gy": ring[dy][0], "af": ring[dy][1]} for dx, dy in SIDES}
    af_peer = [(af + k) % 4 for k in range(4)]

    plane = n_y * n_x
    place = row * n_x + col
    kept = 16 // plane
    far = [k for k in FAR if k < plane]

    def at_place(k):
        other = (place + k) % plane
        return other // n_x, high * n_x + other % n_x

    for side in SIDES:
        (fx, cx), (fy, cy) = EDGE[side[0]], EDGE[side[1]]
        field[:, fx : fx + cx, fy : fy + cy] = jnp.zeros((4, cx, cy, 32, 128), BF16)

    barrier = pltpu.get_barrier_semaphore()
    across = [{"gy": high * n_x + (col + k) % n_x} for k in range(1, n_x)]
    across += [{"gy": (1 - high) * n_x + col}]
    partners = across + [{"af": af_peer[k]} for k in range(1, 4)]
    partners += [{"gx": 2 * ((row + k) % n_y) + core} for k in range(1, n_y)]
    half = col % 2
    buddy = gy + 1 - 2 * half
    sharers = [{"gx": 2 * row + 1 - core, "gy": gy}, {"gx": gx, "gy": buddy}, {"gx": 2 * row + 1 - core, "gy": buddy}]
    partners.append(sharers[2])
    for dx, dy in SIDES:
        partners.append({"gx": (gx + dx + n_gx) % n_gx, "gy": ring[dy][0], "af": ring[dy][1]})
    for partner in partners:
        pl.semaphore_signal(barrier, inc=1, device_id=partner, device_id_type=MESH)

    r, q = iota((128, 128), 0), iota((128, 128), 1)
    to_wire = jnp.where(q == (r % 8) * 16 + r // 8, 1.0, 0.0).astype(BF16)
    from_wire = jnp.where(q == (r % 16) * 8 + r // 16, 1.0, 0.0).astype(BF16)

    def stage_input(which, source):
        block = jnp.concatenate([source[:, x].reshape(128, 128) for x in range(4)], axis=1)
        moved = jnp.dot(to_wire, block, preferred_element_type=F32).astype(BF16)
        for x in range(4):
            for j in range(4):
                part = moved[32 * j : 32 * j + 32, 128 * x : 128 * x + 128]
                stage[which, j, x] = part.reshape(2, 16, 128)
        got[which, pl.ds(af, 1)] = stage[which, pl.ds(sub, 1)]

    def in_copy(which, k):
        return pltpu.make_async_remote_copy(
            src_ref=stage.at[which, sub_of(af_peer[k], gy)],
            dst_ref=got.at[which, af],
            send_sem=in_send.at[which, k],
            recv_sem=in_recv.at[which, k],
            device_id={"af": af_peer[k]},
            device_id_type=MESH,
        )

    def w_copy(k):
        return pltpu.make_async_remote_copy(
            src_ref=w_stage.at[core, half],
            dst_ref=w_got.at[af, core, half],
            send_sem=w_send.at[k],
            recv_sem=w_recv.at[k],
            device_id={"af": af_peer[k]},
            device_id_type=MESH,
        )

    def pass_copy(k, to):
        origin = (af + 4 - k) % 4
        return pltpu.make_async_remote_copy(
            src_ref=w_got.at[origin, core, half],
            dst_ref=w_got.at[origin, core, half],
            send_sem=pass_send.at[k, to],
            recv_sem=pass_recv.at[k, to],
            device_id=sharers[to],
            device_id_type=MESH,
        )

    loads[0].wait()
    stage_input(VOL, vol)
    for load in loads[1:]:
        load.wait()
    diag = iota((8, 8), 0) == iota((8, 8), 1)
    bias_col = jnp.sum(jnp.where(diag, bias[...], 0.0), axis=1, keepdims=True)
    part_a = bias_col.astype(BF16).astype(F32)
    part_b = (bias_col - part_a).astype(BF16).astype(F32)
    part_c = (bias_col - part_a) - part_b
    lane32 = iota((8, 32), 1)
    spare = jnp.where(lane32 == 0, part_a, jnp.where(lane32 == 1, part_b, jnp.where(lane32 == 2, part_c, 0.0)))
    for which, weight in enumerate((w_one, w_two)):
        groups = []
        for a in range(7):
            taps = []
            for b in range(4):
                t = 4 * a + b
                taps.append(weight[t // 9, (t // 3) % 3, t % 3].astype(F32) if t < 27 else spare)
            groups.append(jnp.concatenate(taps, axis=1))
        groups.append(jnp.zeros((8, 128), F32))
        packed = jnp.concatenate(groups, axis=0).astype(BF16)
        w_stage[which] = packed.reshape(2, 32, 128)
        w_got[af, which] = packed.reshape(2, 32, 128)
    pl.semaphore_wait(barrier, len(partners))
    for k in (2, 1, 3):
        in_copy(VOL, k).start()
    for partner in across:
        pl.semaphore_signal(line_in, inc=1, device_id=partner, device_id_type=MESH)

    for k in (2, 1, 3):
        w_copy(k).start()
    stage_input(COT, cot)
    for k in (2, 1, 3):
        in_copy(VOL, k).wait_send()
    for k in (2, 1, 3):
        in_copy(COT, k).start()

    def halo_copy(which, side):
        number = SIDES.index(side)
        (sx, nx), (sy, ny) = SEND[side[0]], SEND[side[1]]
        (lx, _), (ly, _) = LAND[side[0]], LAND[side[1]]
        return pltpu.make_async_remote_copy(
            src_ref=field.at[which, sx : sx + nx, sy : sy + ny],
            dst_ref=field.at[which, lx : lx + nx, ly : ly + ny],
            send_sem=halo_send.at[which, number],
            recv_sem=halo_recv.at[which, number],
            device_id=neighbour[side],
            device_id_type=MESH,
        )

    def halo_start(which):
        for side in SIDES:

            @pl.when(has(*side))
            def _(side=side):
                halo_copy(which, side).start()

    def halo_wait(which):
        for side in SIDES:

            @pl.when(has(-side[0], -side[1]))
            def _(side=side):
                halo_copy(which, side).wait_recv()

    def assemble(which):
        for x in range(4):
            for pair in range(2):
                parts = [got[which, s, x, pair].astype(F32) for s in range(4)]
                for odd in range(2):
                    rows = [part[8 * odd : 8 * odd + 8] for part in parts]
                    field[which, 1 + x, 1 + 2 * pair + odd] = jnp.concatenate(rows, axis=0).astype(BF16)

    for k in range(1, 4):
        in_copy(VOL, k).wait_recv()
    assemble(VOL)
    halo_start(VOL)

    for k in range(1, 4):
        w_copy(k).wait_recv()
        for to in (1, 2, 0):
            pass_copy(k, to).start()
    for k in range(1, 4):
        in_copy(COT, k).wait_recv()
    assemble(COT)
    halo_start(COT)
    for k in range(1, 4):
        for to in range(3):
            pass_copy(k, to).wait_recv()

    def taps_of(which):
        parts = [w_got[s, which].reshape(64, 128).astype(F32) for s in range(4)]
        groups = [
            jnp.concatenate([part[8 * a : 8 * a + 8] for part in parts], axis=0) for a in range(7)
        ]

        def tap(dx, dy, dz):
            t = (dx * 3 + dy) * 3 + dz
            return groups[t // 4][:, 32 * (t % 4) : 32 * (t % 4) + 32]

        return groups, tap

    def make_forward(which):
        groups, tap = taps_of(which)
        for dz in range(3):
            line = jnp.concatenate([tap(k // 3, k % 3, dz) for k in range(9)], axis=1)
            lhs[2 * which, 32 * dz : 32 * dz + 32] = line.astype(BF16)
        return groups

    def make_turned(which):
        _, tap = taps_of(which)
        zeros = jnp.zeros((32, 32), F32)
        for dx in range(3):
            lines = [
                jnp.concatenate([tap(2 - dx, 2 - dy, 2 - dz) for dz in range(3)] + [zeros], axis=1)
                for dy in range(3)
            ]
            lines.append(jnp.zeros((32, 128), F32))
            block = jnp.concatenate(lines, axis=0)
            lhs[2 * which + 1, :, 96 * dx : 96 * dx + 96] = block.T[:96, :96].astype(BF16)

    groups = make_forward(0)
    bias_all = groups[6][:, 96:97] + groups[6][:, 97:98] + groups[6][:, 98:99]
    make_turned(1)

    lane = iota((32, 128), 1)
    not_first = lane > 0
    not_last = lane < 127

    def shift_up(rows):
        return jnp.where(not_first, pltpu.roll(rows, 1, 1), 0.0)

    def shift_down(rows):
        return jnp.where(not_last, pltpu.roll(rows, 127, 1), 0.0)

    def window(which, x, dx):
        return jnp.concatenate(
            [field[which, x + dx, y : y + 3].reshape(96, 128) for y in range(4)], axis=1
        )

    def conv(which, number, x):
        block = jnp.concatenate([window(which, x, dx) for dx in range(3)], axis=0)
        sums = jnp.dot(lhs[number], block, preferred_element_type=F32)
        lines = []
        for y in range(4):
            part = sums[:, 128 * y : 128 * y + 128]
            lines.append(part[32:64] + shift_up(part[0:32]) + shift_down(part[64:96]))
        return lines

    halo_wait(VOL)
    for x in range(4):
        for y, line in enumerate(conv(VOL, 0, x)):
            act = line + bias_all
            pre_act[x, y] = act
            field[HID, 1 + x, 1 + y] = (act / (1.0 + jnp.exp(-act))).astype(BF16)
    halo_start(HID)

    make_forward(1)
    make_turned(0)
    halo_wait(COT)
    bias_sum = jnp.zeros((32, 128), F32)
    for x in range(4):
        for y, line in enumerate(conv(COT, 3, x)):
            act = pre_act[x, y]
            sig = 1.0 / (1.0 + jnp.exp(-act))
            value = (line * sig * (1.0 + act * (1.0 - sig))).astype(BF16)
            bias_sum = bias_sum + value.astype(F32)
            field[PRE, 1 + x, 1 + y] = value
    halo_start(PRE)

    def shifted(which, x, flip):
        columns = []
        for y in range(4):
            rows = field[which, 1 + x, 1 + y].astype(F32)
            up, down = shift_up(rows), shift_down(rows)
            trio = [down, rows, up] if flip else [up, rows, down]
            columns.append(jnp.concatenate(trio, axis=0).astype(BF16))
        return jnp.concatenate(columns, axis=1)

    along = (((1,), (1,)), ((), ()))

    acc_one = [jnp.zeros((96, 96), F32) for _ in range(3)]
    acc_two = [jnp.zeros((96, 96), F32) for _ in range(3)]
    for x in range(4):
        own_pre = shifted(PRE, x, True)
        own_hid = shifted(HID, x, False)
        for dx in range(3):
            acc_one[dx] = acc_one[dx] + lax.dot_general(
                own_pre, window(VOL, x, dx), along, preferred_element_type=F32
            )
            acc_two[dx] = acc_two[dx] + lax.dot_general(
                window(COT, x, dx), own_hid, along, preferred_element_type=F32
            )
    bias_own = jnp.sum(bias_sum, axis=1, keepdims=True)
    for which, acc in enumerate((acc_one, acc_two)):
        for s in range(4):
            blocks = [acc[k // 3][32 * (k % 3) + 8 * s : 32 * (k % 3) + 8 * s + 8] for k in range(9)]
            tiles = []
            for k in range(6):
                cut = blocks[6 + k // 3][:, 32 * (k % 3) : 32 * (k % 3) + 32]
                tiles.append(jnp.concatenate([blocks[k], cut], axis=1))
            if which == 0:
                extra = jnp.broadcast_to(bias_own[8 * s : 8 * s + 8], (8, 32))
            else:
                extra = jnp.zeros((8, 32), F32)
            tiles.append(jnp.concatenate([blocks[8], extra], axis=1))
            tiles.append(jnp.zeros((8, 128), F32))
            for k in range(8):
                grad[which, 2 * k, s] = tiles[k][0:4]
                grad[which, 2 * k + 1, s] = tiles[k][4:8]

    core_copy = pltpu.make_async_remote_copy(
        src_ref=grad.at[1 - core],
        dst_ref=core_got,
        send_sem=core_send.at[0],
        recv_sem=core_recv.at[0],
        device_id={"gx": 2 * row + 1 - core},
        device_id_type=MESH,
    )
    core_copy.start()

    def out_copy(which, k):
        return pltpu.make_async_remote_copy(
            src_ref=out_stage.at[which, af_peer[k]],
            dst_ref=out_got.at[which, sub],
            send_sem=out_send.at[which, k],
            recv_sem=out_recv.at[which, k],
            device_id={"af": af_peer[k]},
            device_id_type=MESH,
        )

    def produce(which, source, number):
        for x in range(4):
            lines = conv(source, number, x)
            for pair in range(2):
                for s in range(4):
                    rows = [lines[2 * pair + odd][8 * s : 8 * s + 8] for odd in range(2)]
                    out_stage[which, s, x, pair] = jnp.concatenate(rows, axis=0).astype(BF16)
        out_got[which, pl.ds(sub, 1)] = out_stage[which, pl.ds(af, 1)]
        for k in (2, 1, 3):
            out_copy(which, k).start()

    halo_wait(HID)
    produce(0, HID, 2)

    pl.semaphore_wait(line_in, len(across))
    core_copy.wait_recv()
    core_sum[...] = grad[core] + core_got[...]
    plane_got[place] = core_sum[pl.ds(place * kept, kept)]

    def plane_copy(k):
        other_row, other_gy = at_place(k)
        return pltpu.make_async_remote_copy(
            src_ref=core_sum.at[pl.ds(((place + k) % plane) * kept, kept)],
            dst_ref=plane_got.at[place],
            send_sem=plane_send.at[k],
            recv_sem=plane_recv.at[k],
            device_id={"gx": 2 * other_row + core, "gy": other_gy},
            device_id_type=MESH,
        )

    for k in far:
        plane_copy(k).start()

    halo_wait(PRE)
    produce(1, PRE, 1)

    for k in range(1, plane):
        plane_copy(k).wait_recv()
    line_stage[...] = sum([plane_got[i] for i in range(1, plane)], plane_got[0])

    at_line = high * 4 + af
    line_got[core, at_line] = line_stage[:, pl.ds(af, 1)].reshape(kept, 4, 128)

    def line_copy(k, same):
        other = af_peer[k % 4]
        return pltpu.make_async_remote_copy(
            src_ref=line_stage.at[:, other],
            dst_ref=line_got.at[core, at_line],
            send_sem=line_send.at[2 * k + same],
            recv_sem=line_recv.at[2 * k + same],
            device_id={
                "gx": 2 * row + (core if same else 1 - core),
                "gy": ((high + k // 4) % 2) * n_x + col,
                "af": other,
            },
            device_id_type=MESH,
        )

    line_others = [(k, same) for k in (4, 5, 6, 7, 2, 3, 1) for same in (1, 0)] + [(0, 0)]
    for k, same in line_others:
        line_copy(k, same).start()

    def finish(which, target):
        for k in range(1, 4):
            out_copy(which, k).wait_recv()
        block = jnp.concatenate(
            [
                jnp.concatenate([out_got[which, j, x].reshape(32, 128) for j in range(4)], axis=0)
                for x in range(4)
            ],
            axis=1,
        )
        moved = jnp.dot(from_wire, block, preferred_element_type=F32).astype(BF16)
        for x in range(4):
            target[:, x] = moved[:, 128 * x : 128 * x + 128].reshape(8, 16, 128)

    finish(0, out)
    stores[0].start()
    scale = 1.0 / math.sqrt(4 * n_gx * 16 * n_gy * 128)

    def last_copy(k):
        other_row, other_gy = at_place(k)
        part = final.at[place]
        return pltpu.make_async_remote_copy(
            src_ref=part,
            dst_ref=part,
            send_sem=last_send.at[k],
            recv_sem=last_recv.at[k],
            device_id={"gx": 2 * other_row + core, "gy": other_gy},
            device_id_type=MESH,
        )

    for k, same in line_others:
        line_copy(k, same).wait_recv()
    for kind in range(2):
        total = sum([line_got[kind, i] for i in range(1, 8)], line_got[kind, 0])
        final[place, pl.ds(kind * kept, kept)] = total * scale
    for k in far:
        last_copy(k).start()

    finish(1, in_grad)
    stores[1].start()

    for k in range(1, plane):
        last_copy(k).wait_recv()

    stores[2].start()

    for k in range(1, 4):
        in_copy(COT, k).wait_send()
        w_copy(k).wait_send()
        out_copy(0, k).wait_send()
        out_copy(1, k).wait_send()
        for to in range(3):
            pass_copy(k, to).wait_send()
    for which in (VOL, COT, HID, PRE):
        for side in SIDES:

            @pl.when(has(*side))
            def _(which=which, side=side):
                halo_copy(which, side).wait_send()

    core_copy.wait_send()
    for k in range(1, plane):
        plane_copy(k).wait_send()
    for k, same in line_others:
        line_copy(k, same).wait_send()
    for k in range(1, plane):
        last_copy(k).wait_send()
    for copy in stores:
        copy.wait()


def store(
    kept, out_in, in_grad_in, final_in, out_to, in_grad_to, g_one_to, g_bias_to, g_two_to,
    out, in_grad, final, g_one, g_bias, g_two, sems,
):
    loads = [
        pltpu.make_async_copy(source, target, sems.at[0, i])
        for i, (source, target) in enumerate(((final_in, final), (out_in, out), (in_grad_in, in_grad)))
    ]
    stores = [
        pltpu.make_async_copy(source, target, sems.at[1, i])
        for i, (source, target) in enumerate(
            ((out, out_to), (in_grad, in_grad_to), (g_one, g_one_to), (g_bias, g_bias_to), (g_two, g_two_to))
        )
    ]
    for load in loads:
        load.start()
    loads[0].wait()
    diag = iota((8, 8), 0) == iota((8, 8), 1)
    for kind in range(2):
        halves = [final[k // kept, kind * kept + k % kept] for k in range(14)]
        tiles = [jnp.concatenate(halves[2 * k : 2 * k + 2], axis=0) for k in range(7)]
        if kind == 0:
            bias_total = tiles[6][:, 96:97]
        for a in range(3):
            for b in range(3):
                for c in range(3):
                    k = 3 * a + b
                    if k < 6:
                        tap = tiles[k][:, 32 * c : 32 * c + 32]
                    elif k < 8:
                        tap = tiles[3 * (k - 6) + c][:, 96:128]
                    else:
                        tap = tiles[6][:, 32 * c : 32 * c + 32]
                    if kind == 0:
                        g_one[a, c, b] = tap
                    else:
                        g_two[2 - a, 2 - b, c] = tap
    g_bias[...] = jnp.sum(jnp.where(diag, bias_total, 0.0), axis=0, keepdims=True)
    for copy in stores[2:]:
        copy.start()
    for load, copy in zip(loads[1:], stores):
        load.wait()
        copy.start()
    for copy in stores:
        copy.wait()


def body(dims, volume, weight_one, bias_one, weight_two, cotangent):
    plane = (dims[0] // 2) * (dims[1] // 2)
    as_taps = (2, 3, 4, 0, 1)
    dma = pltpu.SemaphoreType.DMA
    cells = jax.ShapeDtypeStruct((8, 4, 16, 128), BF16)
    taps = jax.ShapeDtypeStruct((3, 3, 3, 8, 32), F32)
    dense = jax.ShapeDtypeStruct((plane, 2 * (16 // plane), 4, 128), F32)
    results = pl.pallas_call(
        functools.partial(kernel, dims),
        out_shape=(cells, cells, dense),
        in_specs=[pl.BlockSpec(memory_space=pltpu.HBM)] * 5,
        out_specs=[pl.BlockSpec(memory_space=pltpu.HBM)] * 3,
        scratch_shapes=[
            pltpu.VMEM((8, 4, 16, 128), BF16),
            pltpu.VMEM((8, 4, 16, 128), BF16),
            pltpu.VMEM((8, 4, 16, 128), BF16),
            pltpu.VMEM((3, 3, 3, 8, 32), BF16),
            pltpu.VMEM((1, 8), F32),
            pltpu.VMEM((3, 3, 3, 8, 32), BF16),
            pltpu.VMEM((8, 4, 16, 128), BF16),
            pltpu.VMEM((2, 4, 4, 2, 16, 128), BF16),
            pltpu.VMEM((2, 4, 4, 2, 16, 128), BF16),
            pltpu.VMEM((2, 2, 32, 128), BF16),
            pltpu.VMEM((4, 2, 2, 32, 128), BF16),
            pltpu.VMEM((4, 6, 6, 32, 128), BF16),
            pltpu.VMEM((4, 4, 32, 128), F32),
            pltpu.VMEM((4, 96, 288), BF16),
            pltpu.VMEM((2, 4, 4, 2, 16, 128), BF16),
            pltpu.VMEM((2, 4, 4, 2, 16, 128), BF16),
            pltpu.VMEM((2, 16, 4, 4, 128), F32),
            pltpu.VMEM((16, 4, 4, 128), F32),
            pltpu.VMEM((16, 4, 4, 128), F32),
            pltpu.VMEM((plane, 16 // plane, 4, 4, 128), F32),
            pltpu.VMEM((16 // plane, 4, 4, 128), F32),
            pltpu.VMEM((2, 8, 16 // plane, 4, 128), F32),
            pltpu.VMEM((plane, 2 * (16 // plane), 4, 128), F32),
            dma((2, 4)), dma((2, 4)), dma((4,)), dma((4,)), dma((4, 3)), dma((4, 3)),
            dma((4, 8)), dma((4, 8)), dma((2, 4)), dma((2, 4)),
            dma((1,)), dma((1,)), dma((plane,)), dma((plane,)), dma((16,)), dma((16,)), dma((plane,)), dma((plane,)),
            dma((5,)), dma((3,)), pltpu.SemaphoreType.REGULAR,
        ],
        compiler_params=pltpu.CompilerParams(
            collective_id=0, has_side_effects=True, vmem_limit_bytes=60 * 1024 * 1024
        ),
    )(
        volume,
        jnp.transpose(weight_one, as_taps),
        bias_one.reshape(1, 8),
        jnp.transpose(weight_two, as_taps),
        cotangent,
    )
    given = (cells, cells, taps, jax.ShapeDtypeStruct((1, 8), F32), taps)
    out, in_grad, g_one, g_bias, g_two = pl.pallas_call(
        functools.partial(store, 16 // plane),
        out_shape=given,
        in_specs=[pl.BlockSpec(memory_space=pltpu.HBM)] * 3,
        out_specs=[pl.BlockSpec(memory_space=pltpu.HBM)] * 5,
        scratch_shapes=[pltpu.VMEM(part.shape, part.dtype) for part in (cells, cells, dense, *given[2:])]
        + [dma((2, 5))],
        compiler_params=pltpu.CompilerParams(vmem_limit_bytes=60 * 1024 * 1024),
    )(*results)
    as_given = (3, 4, 0, 1, 2)
    return (
        out,
        in_grad,
        jnp.transpose(g_one, as_given),
        g_bias.reshape(8),
        jnp.transpose(g_two, as_given),
    )


def solution(mesh):
    dims = (mesh.shape["gx"], mesh.shape["gy"])
    return jax.shard_map(
        functools.partial(body, dims),
        mesh=mesh,
        in_specs=(
            P("af", "gx", "gy", None),
            P("af", None, None, None, None),
            P("af"),
            P("af", None, None, None, None),
            P("af", "gx", "gy", None),
        ),
        out_specs=(
            P("af", "gx", "gy", None),
            P("af", "gx", "gy", None),
            P("af", None, None, None, None),
            P("af"),
            P("af", None, None, None, None),
        ),
        check_vma=False,
    )
```

```python
import functools
import math

import jax
import jax.numpy as jnp
from jax import lax
from jax.experimental import pallas as pl
from jax.experimental.pallas import tpu as pltpu
from jax.sharding import PartitionSpec as P

MESH = pl.DeviceIdType.MESH
F32 = jnp.float32
BF16 = jnp.bfloat16

VOL, COT, HID, PRE = 0, 1, 2, 3
SIDES = [(-1, -1), (-1, 1), (1, -1), (1, 1), (0, -1), (0, 1), (-1, 0), (1, 0)]
FAR = (10, 9, 11, 6, 14, 8, 2, 5, 7, 13, 15, 1, 3, 4, 12)
SEND = {-1: (1, 1), 0: (1, 4), 1: (4, 1)}
EDGE = {-1: (0, 1), 0: (1, 4), 1: (5, 1)}
LAND = {-1: (5, 1), 0: (1, 4), 1: (0, 1)}


def iota(shape, dim):
    return lax.broadcasted_iota(jnp.int32, shape, dim)


def kernel(
    dims,
    vol_in, w_one_in, bias_in, w_two_in, cot_in,
    out_to, in_grad_to, final_to,
    out, in_grad,
    vol, w_one, bias, w_two, cot,
    stage, got, w_stage, w_got, field, pre_act, lhs,
    out_stage, out_got, grad, core_got, core_sum, plane_got, line_stage, line_got, final,
    in_send, in_recv, w_send, w_recv, pass_send, pass_recv, halo_send, halo_recv, out_send, out_recv,
    core_send, core_recv, plane_send, plane_recv, line_send, line_recv, last_send, last_recv, load_sem, store_sem, line_in,
):
    loads = [
        pltpu.make_async_copy(source, target, load_sem.at[i])
        for i, (source, target) in enumerate(
            ((vol_in, vol), (w_one_in, w_one), (w_two_in, w_two), (bias_in, bias), (cot_in, cot))
        )
    ]
    for load in loads:
        load.start()
    stores = [
        pltpu.make_async_copy(source, target, store_sem.at[i])
        for i, (source, target) in enumerate(
            ((out, out_to), (in_grad, in_grad_to), (final, final_to))
        )
    ]
    n_gx, n_gy = dims
    n_y, n_x = n_gx // 2, n_gy // 2
    gx, gy, af = lax.axis_index("gx"), lax.axis_index("gy"), lax.axis_index("af")
    row, core = gx // 2, gx % 2
    col, high = gy % n_x, gy // n_x

    def turned(at):
        even = (at % 2) == 0
        upper = at >= n_x
        return jnp.logical_xor(even, upper)

    def sub_of(at_af, at_gy):
        return jnp.where(turned(at_gy), 3 - at_af, at_af)

    sub = sub_of(af, gy)

    def y_neighbour(step):
        if step == 0:
            return gy, af
        inside = (sub < 3) if step > 0 else (sub > 0)
        gy_new = jnp.where(inside, gy, (gy + step + n_gy) % n_gy)
        sub_new = jnp.where(inside, sub + step, 0 if step > 0 else 3)
        return gy_new, sub_of(sub_new, gy_new)

    def has(dx, dy):
        checks = []
        if dx < 0:
            checks.append(gx > 0)
        if dx > 0:
            checks.append(gx < n_gx - 1)
        if dy < 0:
            checks.append(jnp.logical_or(gy > 0, sub > 0))
        if dy > 0:
            checks.append(jnp.logical_or(gy < n_gy - 1, sub < 3))
        if len(checks) == 1:
            return checks[0]
        return jnp.logical_and(checks[0], checks[1])

    ring = {step: y_neighbour(step) for step in (-1, 0, 1)}
    neighbour = {(dx, dy): {"gx": gx + dx, "gy": ring[dy][0], "af": ring[dy][1]} for dx, dy in SIDES}
    af_peer = [(af + k) % 4 for k in range(4)]

    plane = n_y * n_x
    place = row * n_x + col
    kept = 16 // plane
    far = [k for k in FAR if k < plane]

    def at_place(k):
        other = (place + k) % plane
        return other // n_x, high * n_x + other % n_x

    for side in SIDES:
        (fx, cx), (fy, cy) = EDGE[side[0]], EDGE[side[1]]
        field[:, fx : fx + cx, fy : fy + cy] = jnp.zeros((4, cx, cy, 32, 128), BF16)

    barrier = pltpu.get_barrier_semaphore()
    across = [{"gy": high * n_x + (col + k) % n_x} for k in range(1, n_x)]
    across += [{"gy": (1 - high) * n_x + col}]
    partners = across + [{"af": af_peer[k]} for k in range(1, 4)]
    partners += [{"gx": 2 * ((row + k) % n_y) + core} for k in range(1, n_y)]
    half = col % 2
    buddy = gy + 1 - 2 * half
    sharers = [{"gx": 2 * row + 1 - core, "gy": gy}, {"gx": gx, "gy": buddy}, {"gx": 2 * row + 1 - core, "gy": buddy}]
    partners.append(sharers[2])
    for dx, dy in SIDES:
        partners.append({"gx": (gx + dx + n_gx) % n_gx, "gy": ring[dy][0], "af": ring[dy][1]})
    for partner in partners:
        pl.semaphore_signal(barrier, inc=1, device_id=partner, device_id_type=MESH)

    r, q = iota((128, 128), 0), iota((128, 128), 1)
    to_wire = jnp.where(q == (r % 8) * 16 + r // 8, 1.0, 0.0).astype(BF16)
    from_wire = jnp.where(q == (r % 16) * 8 + r // 16, 1.0, 0.0).astype(BF16)

    def stage_input(which, source):
        block = jnp.concatenate([source[:, x].reshape(128, 128) for x in range(4)], axis=1)
        moved = jnp.dot(to_wire, block, preferred_element_type=F32).astype(BF16)
        for x in range(4):
            for j in range(4):
                part = moved[32 * j : 32 * j + 32, 128 * x : 128 * x + 128]
                stage[which, j, x] = part.reshape(2, 16, 128)
        got[which, pl.ds(af, 1)] = stage[which, pl.ds(sub, 1)]

    def in_copy(which, k):
        return pltpu.make_async_remote_copy(
            src_ref=stage.at[which, sub_of(af_peer[k], gy)],
            dst_ref=got.at[which, af],
            send_sem=in_send.at[which, k],
            recv_sem=in_recv.at[which, k],
            device_id={"af": af_peer[k]},
            device_id_type=MESH,
        )

    def w_copy(k):
        return pltpu.make_async_remote_copy(
            src_ref=w_stage.at[core, half],
            dst_ref=w_got.at[af, core, half],
            send_sem=w_send.at[k],
            recv_sem=w_recv.at[k],
            device_id={"af": af_peer[k]},
            device_id_type=MESH,
        )

    def pass_copy(k, to):
        origin = (af + 4 - k) % 4
        return pltpu.make_async_remote_copy(
            src_ref=w_got.at[origin, core, half],
            dst_ref=w_got.at[origin, core, half],
            send_sem=pass_send.at[k, to],
            recv_sem=pass_recv.at[k, to],
            device_id=sharers[to],
            device_id_type=MESH,
        )

    loads[0].wait()
    stage_input(VOL, vol)
    for load in loads[1:]:
        load.wait()
    diag = iota((8, 8), 0) == iota((8, 8), 1)
    bias_col = jnp.sum(jnp.where(diag, bias[...], 0.0), axis=1, keepdims=True)
    part_a = bias_col.astype(BF16).astype(F32)
    part_b = (bias_col - part_a).astype(BF16).astype(F32)
    part_c = (bias_col - part_a) - part_b
    lane32 = iota((8, 32), 1)
    spare = jnp.where(lane32 == 0, part_a, jnp.where(lane32 == 1, part_b, jnp.where(lane32 == 2, part_c, 0.0)))
    for which, weight in enumerate((w_one, w_two)):
        groups = []
        for a in range(7):
            taps = []
            for b in range(4):
                t = 4 * a + b
                taps.append(weight[t // 9, (t // 3) % 3, t % 3].astype(F32) if t < 27 else spare)
            groups.append(jnp.concatenate(taps, axis=1))
        groups.append(jnp.zeros((8, 128), F32))
        packed = jnp.concatenate(groups, axis=0).astype(BF16)
        w_stage[which] = packed.reshape(2, 32, 128)
        w_got[af, which] = packed.reshape(2, 32, 128)
    pl.semaphore_wait(barrier, len(partners))
    for k in (2, 1, 3):
        in_copy(VOL, k).start()
    for partner in across:
        pl.semaphore_signal(line_in, inc=1, device_id=partner, device_id_type=MESH)

    for k in (2, 1, 3):
        w_copy(k).start()
    stage_input(COT, cot)
    for k in (2, 1, 3):
        in_copy(VOL, k).wait_send()
    for k in (2, 1, 3):
        in_copy(COT, k).start()

    def halo_copy(which, side):
        number = SIDES.index(side)
        (sx, nx), (sy, ny) = SEND[side[0]], SEND[side[1]]
        (lx, _), (ly, _) = LAND[side[0]], LAND[side[1]]
        return pltpu.make_async_remote_copy(
            src_ref=field.at[which, sx : sx + nx, sy : sy + ny],
            dst_ref=field.at[which, lx : lx + nx, ly : ly + ny],
            send_sem=halo_send.at[which, number],
            recv_sem=halo_recv.at[which, number],
            device_id=neighbour[side],
            device_id_type=MESH,
        )

    def halo_start(which):
        for side in SIDES:

            @pl.when(has(*side))
            def _(side=side):
                halo_copy(which, side).start()

    def halo_wait(which):
        for side in SIDES:

            @pl.when(has(-side[0], -side[1]))
            def _(side=side):
                halo_copy(which, side).wait_recv()

    def assemble(which):
        for x in range(4):
            for pair in range(2):
                parts = [got[which, s, x, pair].astype(F32) for s in range(4)]
                for odd in range(2):
                    rows = [part[8 * odd : 8 * odd + 8] for part in parts]
                    field[which, 1 + x, 1 + 2 * pair + odd] = jnp.concatenate(rows, axis=0).astype(BF16)

    for k in range(1, 4):
        in_copy(VOL, k).wait_recv()
    assemble(VOL)
    halo_start(VOL)

    for k in range(1, 4):
        w_copy(k).wait_recv()
        for to in (1, 2, 0):
            pass_copy(k, to).start()
    for k in range(1, 4):
        in_copy(COT, k).wait_recv()
    assemble(COT)
    halo_start(COT)
    for k in range(1, 4):
        for to in range(3):
            pass_copy(k, to).wait_recv()

    def taps_of(which):
        parts = [w_got[s, which].reshape(64, 128).astype(F32) for s in range(4)]
        groups = [
            jnp.concatenate([part[8 * a : 8 * a + 8] for part in parts], axis=0) for a in range(7)
        ]

        def tap(dx, dy, dz):
            t = (dx * 3 + dy) * 3 + dz
            return groups[t // 4][:, 32 * (t % 4) : 32 * (t % 4) + 32]

        return groups, tap

    def make_forward(which):
        groups, tap = taps_of(which)
        for dz in range(3):
            line = jnp.concatenate([tap(k // 3, k % 3, dz) for k in range(9)], axis=1)
            lhs[2 * which, 32 * dz : 32 * dz + 32] = line.astype(BF16)
        return groups

    def make_turned(which):
        _, tap = taps_of(which)
        zeros = jnp.zeros((32, 32), F32)
        for dx in range(3):
            lines = [
                jnp.concatenate([tap(2 - dx, 2 - dy, 2 - dz) for dz in range(3)] + [zeros], axis=1)
                for dy in range(3)
            ]
            lines.append(jnp.zeros((32, 128), F32))
            block = jnp.concatenate(lines, axis=0)
            lhs[2 * which + 1, :, 96 * dx : 96 * dx + 96] = block.T[:96, :96].astype(BF16)

    groups = make_forward(0)
    bias_all = groups[6][:, 96:97] + groups[6][:, 97:98] + groups[6][:, 98:99]
    make_turned(1)

    lane = iota((32, 128), 1)
    not_first = lane > 0
    not_last = lane < 127

    def shift_up(rows):
        return jnp.where(not_first, pltpu.roll(rows, 1, 1), 0.0)

    def shift_down(rows):
        return jnp.where(not_last, pltpu.roll(rows, 127, 1), 0.0)

    def window(which, x, dx):
        return jnp.concatenate(
            [field[which, x + dx, y : y + 3].reshape(96, 128) for y in range(4)], axis=1
        )

    def conv(which, number, x):
        block = jnp.concatenate([window(which, x, dx) for dx in range(3)], axis=0)
        sums = jnp.dot(lhs[number], block, preferred_element_type=F32)
        lines = []
        for y in range(4):
            part = sums[:, 128 * y : 128 * y + 128]
            lines.append(part[32:64] + shift_up(part[0:32]) + shift_down(part[64:96]))
        return lines

    halo_wait(VOL)
    for x in range(4):
        for y, line in enumerate(conv(VOL, 0, x)):
            act = line + bias_all
            pre_act[x, y] = act
            field[HID, 1 + x, 1 + y] = (act / (1.0 + jnp.exp(-act))).astype(BF16)
    halo_start(HID)

    make_forward(1)
    make_turned(0)
    halo_wait(COT)
    bias_sum = jnp.zeros((32, 128), F32)
    for x in range(4):
        for y, line in enumerate(conv(COT, 3, x)):
            act = pre_act[x, y]
            sig = 1.0 / (1.0 + jnp.exp(-act))
            value = (line * sig * (1.0 + act * (1.0 - sig))).astype(BF16)
            bias_sum = bias_sum + value.astype(F32)
            field[PRE, 1 + x, 1 + y] = value
    halo_start(PRE)

    def shifted(which, x, flip):
        columns = []
        for y in range(4):
            rows = field[which, 1 + x, 1 + y].astype(F32)
            up, down = shift_up(rows), shift_down(rows)
            trio = [down, rows, up] if flip else [up, rows, down]
            columns.append(jnp.concatenate(trio, axis=0).astype(BF16))
        return jnp.concatenate(columns, axis=1)

    along = (((1,), (1,)), ((), ()))

    acc_one = [jnp.zeros((96, 96), F32) for _ in range(3)]
    acc_two = [jnp.zeros((96, 96), F32) for _ in range(3)]
    for x in range(4):
        own_pre = shifted(PRE, x, True)
        own_hid = shifted(HID, x, False)
        for dx in range(3):
            acc_one[dx] = acc_one[dx] + lax.dot_general(
                own_pre, window(VOL, x, dx), along, preferred_element_type=F32
            )
            acc_two[dx] = acc_two[dx] + lax.dot_general(
                window(COT, x, dx), own_hid, along, preferred_element_type=F32
            )
    bias_own = jnp.sum(bias_sum, axis=1, keepdims=True)
    for which, acc in enumerate((acc_one, acc_two)):
        for s in range(4):
            blocks = [acc[k // 3][32 * (k % 3) + 8 * s : 32 * (k % 3) + 8 * s + 8] for k in range(9)]
            tiles = []
            for k in range(6):
                cut = blocks[6 + k // 3][:, 32 * (k % 3) : 32 * (k % 3) + 32]
                tiles.append(jnp.concatenate([blocks[k], cut], axis=1))
            if which == 0:
                extra = jnp.broadcast_to(bias_own[8 * s : 8 * s + 8], (8, 32))
            else:
                extra = jnp.zeros((8, 32), F32)
            tiles.append(jnp.concatenate([blocks[8], extra], axis=1))
            tiles.append(jnp.zeros((8, 128), F32))
            for k in range(8):
                grad[which, 2 * k, s] = tiles[k][0:4]
                grad[which, 2 * k + 1, s] = tiles[k][4:8]

    core_copy = pltpu.make_async_remote_copy(
        src_ref=grad.at[1 - core],
        dst_ref=core_got,
        send_sem=core_send.at[0],
        recv_sem=core_recv.at[0],
        device_id={"gx": 2 * row + 1 - core},
        device_id_type=MESH,
    )
    core_copy.start()

    def out_copy(which, k):
        return pltpu.make_async_remote_copy(
            src_ref=out_stage.at[which, af_peer[k]],
            dst_ref=out_got.at[which, sub],
            send_sem=out_send.at[which, k],
            recv_sem=out_recv.at[which, k],
            device_id={"af": af_peer[k]},
            device_id_type=MESH,
        )

    def produce(which, source, number):
        for x in range(4):
            lines = conv(source, number, x)
            for pair in range(2):
                for s in range(4):
                    rows = [lines[2 * pair + odd][8 * s : 8 * s + 8] for odd in range(2)]
                    out_stage[which, s, x, pair] = jnp.concatenate(rows, axis=0).astype(BF16)
        out_got[which, pl.ds(sub, 1)] = out_stage[which, pl.ds(af, 1)]

    def send_out(which):
        for k in (2, 1, 3):
            out_copy(which, k).start()

    halo_wait(HID)
    produce(0, HID, 2)
    send_out(0)

    pl.semaphore_wait(line_in, len(across))
    core_copy.wait_recv()
    core_sum[...] = grad[core] + core_got[...]
    plane_got[place] = core_sum[pl.ds(place * kept, kept)]

    def plane_copy(k):
        other_row, other_gy = at_place(k)
        return pltpu.make_async_remote_copy(
            src_ref=core_sum.at[pl.ds(((place + k) % plane) * kept, kept)],
            dst_ref=plane_got.at[place],
            send_sem=plane_send.at[k],
            recv_sem=plane_recv.at[k],
            device_id={"gx": 2 * other_row + core, "gy": other_gy},
            device_id_type=MESH,
        )

    for k in far:
        plane_copy(k).start()

    halo_wait(PRE)
    produce(1, PRE, 1)

    for k in range(1, plane):
        plane_copy(k).wait_recv()
    line_stage[...] = sum([plane_got[i] for i in range(1, plane)], plane_got[0])

    at_line = high * 4 + af
    line_got[core, at_line] = line_stage[:, pl.ds(af, 1)].reshape(kept, 4, 128)

    def line_copy(k, same):
        other = af_peer[k % 4]
        return pltpu.make_async_remote_copy(
            src_ref=line_stage.at[:, other],
            dst_ref=line_got.at[core, at_line],
            send_sem=line_send.at[2 * k + same],
            recv_sem=line_recv.at[2 * k + same],
            device_id={
                "gx": 2 * row + (core if same else 1 - core),
                "gy": ((high + k // 4) % 2) * n_x + col,
                "af": other,
            },
            device_id_type=MESH,
        )

    line_others = [(k, same) for k in (4, 5, 6, 7, 2, 3, 1) for same in (1, 0)] + [(0, 0)]
    for k, same in line_others:
        line_copy(k, same).start()
    send_out(1)

    def finish(which, target):
        for k in range(1, 4):
            out_copy(which, k).wait_recv()
        block = jnp.concatenate(
            [
                jnp.concatenate([out_got[which, j, x].reshape(32, 128) for j in range(4)], axis=0)
                for x in range(4)
            ],
            axis=1,
        )
        moved = jnp.dot(from_wire, block, preferred_element_type=F32).astype(BF16)
        for x in range(4):
            target[:, x] = moved[:, 128 * x : 128 * x + 128].reshape(8, 16, 128)

    finish(0, out)
    stores[0].start()
    scale = 1.0 / math.sqrt(4 * n_gx * 16 * n_gy * 128)

    def last_copy(k):
        other_row, other_gy = at_place(k)
        part = final.at[place]
        return pltpu.make_async_remote_copy(
            src_ref=part,
            dst_ref=part,
            send_sem=last_send.at[k],
            recv_sem=last_recv.at[k],
            device_id={"gx": 2 * other_row + core, "gy": other_gy},
            device_id_type=MESH,
        )

    for k, same in line_others:
        line_copy(k, same).wait_recv()
    for kind in range(2):
        total = sum([line_got[kind, i] for i in range(1, 8)], line_got[kind, 0])
        final[place, pl.ds(kind * kept, kept)] = total * scale
    for k in far:
        last_copy(k).start()

    finish(1, in_grad)
    stores[1].start()

    for k in range(1, plane):
        last_copy(k).wait_recv()

    stores[2].start()

    for k in range(1, 4):
        in_copy(COT, k).wait_send()
        w_copy(k).wait_send()
        out_copy(0, k).wait_send()
        out_copy(1, k).wait_send()
        for to in range(3):
            pass_copy(k, to).wait_send()
    for which in (VOL, COT, HID, PRE):
        for side in SIDES:

            @pl.when(has(*side))
            def _(which=which, side=side):
                halo_copy(which, side).wait_send()

    core_copy.wait_send()
    for k in range(1, plane):
        plane_copy(k).wait_send()
    for k, same in line_others:
        line_copy(k, same).wait_send()
    for k in range(1, plane):
        last_copy(k).wait_send()
    for copy in stores:
        copy.wait()


def store(
    kept, out_in, in_grad_in, final_in, out_to, in_grad_to, g_one_to, g_bias_to, g_two_to,
    out, in_grad, final, g_one, g_bias, g_two, sems,
):
    loads = [
        pltpu.make_async_copy(source, target, sems.at[0, i])
        for i, (source, target) in enumerate(((final_in, final), (out_in, out), (in_grad_in, in_grad)))
    ]
    stores = [
        pltpu.make_async_copy(source, target, sems.at[1, i])
        for i, (source, target) in enumerate(
            ((out, out_to), (in_grad, in_grad_to), (g_one, g_one_to), (g_bias, g_bias_to), (g_two, g_two_to))
        )
    ]
    for load in loads:
        load.start()
    loads[0].wait()
    diag = iota((8, 8), 0) == iota((8, 8), 1)
    for kind in range(2):
        halves = [final[k // kept, kind * kept + k % kept] for k in range(14)]
        tiles = [jnp.concatenate(halves[2 * k : 2 * k + 2], axis=0) for k in range(7)]
        if kind == 0:
            bias_total = tiles[6][:, 96:97]
        for a in range(3):
            for b in range(3):
                for c in range(3):
                    k = 3 * a + b
                    if k < 6:
                        tap = tiles[k][:, 32 * c : 32 * c + 32]
                    elif k < 8:
                        tap = tiles[3 * (k - 6) + c][:, 96:128]
                    else:
                        tap = tiles[6][:, 32 * c : 32 * c + 32]
                    if kind == 0:
                        g_one[a, c, b] = tap
                    else:
                        g_two[2 - a, 2 - b, c] = tap
    g_bias[...] = jnp.sum(jnp.where(diag, bias_total, 0.0), axis=0, keepdims=True)
    for copy in stores[2:]:
        copy.start()
    for load, copy in zip(loads[1:], stores):
        load.wait()
        copy.start()
    for copy in stores:
        copy.wait()


def body(dims, volume, weight_one, bias_one, weight_two, cotangent):
    plane = (dims[0] // 2) * (dims[1] // 2)
    as_taps = (2, 3, 4, 0, 1)
    dma = pltpu.SemaphoreType.DMA
    cells = jax.ShapeDtypeStruct((8, 4, 16, 128), BF16)
    taps = jax.ShapeDtypeStruct((3, 3, 3, 8, 32), F32)
    dense = jax.ShapeDtypeStruct((plane, 2 * (16 // plane), 4, 128), F32)
    results = pl.pallas_call(
        functools.partial(kernel, dims),
        out_shape=(cells, cells, dense),
        in_specs=[pl.BlockSpec(memory_space=pltpu.HBM)] * 5,
        out_specs=[pl.BlockSpec(memory_space=pltpu.HBM)] * 3,
        scratch_shapes=[
            pltpu.VMEM((8, 4, 16, 128), BF16),
            pltpu.VMEM((8, 4, 16, 128), BF16),
            pltpu.VMEM((8, 4, 16, 128), BF16),
            pltpu.VMEM((3, 3, 3, 8, 32), BF16),
            pltpu.VMEM((1, 8), F32),
            pltpu.VMEM((3, 3, 3, 8, 32), BF16),
            pltpu.VMEM((8, 4, 16, 128), BF16),
            pltpu.VMEM((2, 4, 4, 2, 16, 128), BF16),
            pltpu.VMEM((2, 4, 4, 2, 16, 128), BF16),
            pltpu.VMEM((2, 2, 32, 128), BF16),
            pltpu.VMEM((4, 2, 2, 32, 128), BF16),
            pltpu.VMEM((4, 6, 6, 32, 128), BF16),
            pltpu.VMEM((4, 4, 32, 128), F32),
            pltpu.VMEM((4, 96, 288), BF16),
            pltpu.VMEM((2, 4, 4, 2, 16, 128), BF16),
            pltpu.VMEM((2, 4, 4, 2, 16, 128), BF16),
            pltpu.VMEM((2, 16, 4, 4, 128), F32),
            pltpu.VMEM((16, 4, 4, 128), F32),
            pltpu.VMEM((16, 4, 4, 128), F32),
            pltpu.VMEM((plane, 16 // plane, 4, 4, 128), F32),
            pltpu.VMEM((16 // plane, 4, 4, 128), F32),
            pltpu.VMEM((2, 8, 16 // plane, 4, 128), F32),
            pltpu.VMEM((plane, 2 * (16 // plane), 4, 128), F32),
            dma((2, 4)), dma((2, 4)), dma((4,)), dma((4,)), dma((4, 3)), dma((4, 3)),
            dma((4, 8)), dma((4, 8)), dma((2, 4)), dma((2, 4)),
            dma((1,)), dma((1,)), dma((plane,)), dma((plane,)), dma((16,)), dma((16,)), dma((plane,)), dma((plane,)),
            dma((5,)), dma((3,)), pltpu.SemaphoreType.REGULAR,
        ],
        compiler_params=pltpu.CompilerParams(
            collective_id=0, has_side_effects=True, vmem_limit_bytes=60 * 1024 * 1024
        ),
    )(
        volume,
        jnp.transpose(weight_one, as_taps),
        bias_one.reshape(1, 8),
        jnp.transpose(weight_two, as_taps),
        cotangent,
    )
    given = (cells, cells, taps, jax.ShapeDtypeStruct((1, 8), F32), taps)
    out, in_grad, g_one, g_bias, g_two = pl.pallas_call(
        functools.partial(store, 16 // plane),
        out_shape=given,
        in_specs=[pl.BlockSpec(memory_space=pltpu.HBM)] * 3,
        out_specs=[pl.BlockSpec(memory_space=pltpu.HBM)] * 5,
        scratch_shapes=[pltpu.VMEM(part.shape, part.dtype) for part in (cells, cells, dense, *given[2:])]
        + [dma((2, 5))],
        compiler_params=pltpu.CompilerParams(vmem_limit_bytes=60 * 1024 * 1024),
    )(*results)
    as_given = (3, 4, 0, 1, 2)
    return (
        out,
        in_grad,
        jnp.transpose(g_one, as_given),
        g_bias.reshape(8),
        jnp.transpose(g_two, as_given),
    )


def solution(mesh):
    dims = (mesh.shape["gx"], mesh.shape["gy"])
    return jax.shard_map(
        functools.partial(body, dims),
        mesh=mesh,
        in_specs=(
            P("af", "gx", "gy", None),
            P("af", None, None, None, None),
            P("af"),
            P("af", None, None, None, None),
            P("af", "gx", "gy", None),
        ),
        out_specs=(
            P("af", "gx", "gy", None),
            P("af", "gx", "gy", None),
            P("af", None, None, None, None),
            P("af"),
            P("af", None, None, None, None),
        ),
        check_vma=False,
    )
```
